128 devices in a mesh: blk: 8 (over y, z_lo), head: 16 (over x, z_hi, core).
Axes of the slice: x: 4, y: 4, z: 4 (z_hi: 2, z_lo: 2; z = z_hi * 2 + z_lo), core: 2. Of those that a mesh axis runs over, the one named last changes fastest.
Arguments:
- queries: bfloat16 [20480, 2048], P(('blk', 'head')), may hold values from -64 to 64
- key_rows: bfloat16 [20480, 2048], P(('blk', 'head')), may hold values from -12 to 12
- value_rows: bfloat16 [20480, 2048], P(('blk', 'head')), may hold values from -6 to 6
- w_out: bfloat16 [2048, 3072], replicated, may hold values from -0.125 to 0.125
- shift_vec: float32 [3072], replicated, may hold values from -3 to 3
- scale_vec: float32 [3072], replicated, may hold values from -3 to 3
- w_final: bfloat16 [3072, 64], replicated, may hold values from -0.109375 to 0.109375
- w_conv: bfloat16 [3, 3, 3, 16, 512], replicated, may hold values from -0.3125 to 0.3125
Outputs:
- decoded: bfloat16 [8, 64, 160, 512], P('blk', None, 'head')
The draws below stay inside these ranges and needn't reach their ends.
All inputs are finite; a program needn't handle non-finite values.
Results may differ from the reference program's by a relative error of at most 0.017.
Values may be sent and summed in bfloat16 or wider, within the bound.
No kernel may reach another device: no remote copies, remote signals or barrier semaphores. Data moves between devices by JAX's collectives and lax.ppermute only.
A program may use at most 448 MiB of HBM per device.

```python
import math
import jax
import jax.numpy as jnp
from jax import lax

D = 3072
H = 16
HD = 128
C_LAT = 16
C_VAE = 512
PW = 80
PH = 32
FRAMES = 8
TOKENS = 20480


def shared_keys(key):
    return 2.0 * jnp.clip(jax.random.normal(key, (TOKENS, H * HD), jnp.float32), -6.0, 6.0)


def draw_key_rows(key, part):
    shared = shared_keys(key)
    return shared.astype(jnp.bfloat16)


def draw_queries(key, part):
    key = jax.random.fold_in(key, 12)
    fresh = jnp.clip(jax.random.normal(key, (TOKENS, H * HD), jnp.float32), -6.0, 6.0)
    return fresh.astype(jnp.bfloat16)


def steps_of(stream_key, dims, shards, least, top_value):
    def one(dim, shards_of):
        heights = jax.random.uniform(jax.random.fold_in(jax.random.fold_in(stream_key, 6), dim), (shards_of,), jnp.float32, least / len(shards), top_value / len(shards))
        return jnp.repeat(jnp.exp(heights), dims[dim] // shards_of).reshape((-1,) + (1,) * (len(dims) - dim - 1))

    gain = one(*shards[0])
    for cut in shards[1:]:
        gain = gain * one(*cut)
    return gain


def gaussian(own_key, shape, deviation, bound, shards=(), held_as=jnp.bfloat16):
    factor_of = steps_of(own_key, shape, shards, -0.22, 0.18) if shards else 1.0
    values = jax.random.normal(own_key, shape, jnp.float32) * deviation * factor_of
    return jnp.minimum(jnp.maximum(values, -bound), bound).astype(held_as)


def setup_inputs(seed: int = 0) -> dict:
    key_of = jax.random.split(jax.random.key(seed), 9)
    queries = draw_queries(jax.random.fold_in(key_of[8], 71), 0)
    key_rows = draw_key_rows(jax.random.fold_in(key_of[8], 71), 0)
    value_rows = gaussian(key_of[2], (TOKENS, H * HD), 1.0, 6.0, ((0, 128),))
    w_out = gaussian(key_of[3], (H * HD, D), (H * HD) ** -0.5, 0.125)
    shift_vec = gaussian(key_of[4], (D,), 0.5, 3.0, (), jnp.float32)
    scale_vec = gaussian(key_of[5], (D,), 0.5, 3.0, (), jnp.float32)
    w_final = gaussian(key_of[6], (D, 4 * C_LAT), D ** -0.5, 0.109375)
    w_conv = gaussian(key_of[7], (3, 3, 3, C_LAT, C_VAE), (27 * C_LAT) ** -0.5, 0.3125)
    return {"queries": queries, "key_rows": key_rows, "value_rows": value_rows, "w_out": w_out, "shift_vec": shift_vec, "scale_vec": scale_vec, "w_final": w_final, "w_conv": w_conv}


def attention_head(triple):
    q_head, k_head, v_head = triple
    q_block = math.gcd(TOKENS, 2048)
    q_split = q_head.reshape(TOKENS // q_block, q_block, HD)

    def one_block(q_rows):
        scores = jnp.dot(q_rows, k_head.T, preferred_element_type=jnp.float32) * HD ** (-0.5)
        row_max = lax.optimization_barrier(jnp.max(scores, axis=-1, keepdims=True))
        exp_scores = jnp.exp(scores - row_max)
        weight_sum = lax.optimization_barrier(jnp.sum(exp_scores, axis=-1, keepdims=True))
        weights = exp_scores.astype(jnp.bfloat16)
        result = jnp.dot(weights, v_head, preferred_element_type=jnp.float32) / weight_sum
        return result.astype(jnp.bfloat16)
    return lax.map(one_block, q_split).reshape(TOKENS, HD)

def unfold_window(window, rows_out, cols_out):
    columns = []
    for step_t in range(3):
        for step_y in range(3):
            for step_x in range(3):
                columns.append(window[step_t, step_y:step_y + rows_out, step_x:step_x + cols_out, :])
    return jnp.concatenate(columns, axis=-1).reshape(rows_out * cols_out, -1)

def reference(queries, key_rows, value_rows, w_out, shift_vec, scale_vec, w_final, w_conv):
    q_heads = queries.reshape(TOKENS, H, HD).transpose(1, 0, 2)
    k_heads = key_rows.reshape(TOKENS, H, HD).transpose(1, 0, 2)
    v_heads = value_rows.reshape(TOKENS, H, HD).transpose(1, 0, 2)
    attended = lax.map(attention_head, (q_heads, k_heads, v_heads))
    attended = attended.transpose(1, 0, 2).reshape(TOKENS, H * HD)
    projected = jnp.dot(attended, w_out, preferred_element_type=jnp.float32)
    row_mean = lax.optimization_barrier(jnp.mean(projected, axis=-1, keepdims=True))
    centered = projected - row_mean
    row_var = lax.optimization_barrier(jnp.mean(centered * centered, axis=-1, keepdims=True))
    normed = centered / jnp.sqrt(row_var + 1e-06) * (1.0 + scale_vec) + shift_vec
    normed = normed.astype(jnp.bfloat16)
    patches = jnp.dot(normed, w_final, preferred_element_type=jnp.float32).astype(jnp.bfloat16)
    latent = patches.reshape(FRAMES, PH, PW, C_LAT, 2, 2).transpose(0, 1, 4, 2, 5, 3)
    latent = latent.reshape(FRAMES, 2 * PH, 2 * PW, C_LAT)
    timed = jnp.concatenate([latent[:1], latent[:1], latent], axis=0)
    padded = jnp.pad(timed, ((0, 0), (1, 1), (1, 1), (0, 0)))
    kernel = w_conv.reshape(27 * C_LAT, C_VAE)

    def one_frame(frame_no):
        window = lax.dynamic_slice_in_dim(padded, frame_no, 3, 0)
        columns = unfold_window(window, 2 * PH, 2 * PW)
        result = jnp.dot(columns, kernel, preferred_element_type=jnp.float32)
        return result.astype(jnp.bfloat16).reshape(2 * PH, 2 * PW, C_VAE)
    return lax.map(one_frame, jnp.arange(FRAMES, dtype=jnp.int32))
```

```python
import functools

import jax
import jax.numpy as jnp
import numpy as np
from jax import lax
from jax.experimental import pallas as pl
from jax.experimental.pallas import tpu as pltpu
from jax.sharding import Mesh, PartitionSpec as P

HD = 128
HEADS = 16
D = 3072
C_LAT = 16
C_VAE = 512
PW = 80
PH = 32
BANDS = 16
BAND = 5
WIDE = 8
AXES = ("y", "zl", "x", "zh", "c")
SIZES = (4, 2, 4, 2, 2)
PLANE = ("zl", "x", "zh")
SCALE_LOG2 = HD ** -0.5 * 1.4426950408889634
LIMIT = 1e30
NT = (((1,), (1,)), ((), ()))
STATE = HD + 16
MIB = 2 ** 20
ATTEND_MIB = 36


def dot_nt(a, b):
    return lax.dot_general(a, b, NT, preferred_element_type=jnp.float32)


def attention_kernel(*refs, pieces, first, filled):
    q_ref = refs[0]
    kv_refs = refs[1 : 1 + pieces]
    rest = refs[1 + pieces :]
    if filled:
        rest = rest[1:]
    if first:
        out_ref, vt_ref = rest
    else:
        in_ref, out_ref, vt_ref = rest
    starts = [0]
    for kv in kv_refs:
        starts.append(starts[-1] + kv.shape[0])

    @pl.when(pl.program_id(0) == 0)
    def _():
        for n, kv in enumerate(kv_refs):
            vt_ref[:, starts[n] : starts[n + 1]] = kv[:, HD:].T

    q_scaled = q_ref[...].astype(jnp.float32) * SCALE_LOG2
    q_hi = q_scaled.astype(jnp.bfloat16)
    q_lo = (q_scaled - q_hi.astype(jnp.float32)).astype(jnp.bfloat16)
    q_pair = jnp.concatenate([q_hi, q_lo], axis=1)
    cols = q_pair.shape[0]

    def scores_of(keys):
        return dot_nt(jnp.concatenate([keys, keys], axis=1), q_pair)

    if first:
        reference = jnp.max(scores_of(kv_refs[0][0:256, :HD]), axis=0, keepdims=True)
        total = jnp.zeros((8, cols), jnp.float32)
        acc = jnp.zeros((HD, cols), jnp.float32)
    else:
        reference = in_ref[HD + 8 : HD + 9, :]
        total = in_ref[HD : HD + 8, :]
        acc = in_ref[0:HD, :]
    for n, kv in enumerate(kv_refs):
        size = kv.shape[0]
        step = min(size, 1280)
        for at in range(0, size, step):
            weights = jnp.exp2(scores_of(kv[at : at + step, :HD]) - reference)
            total = total + jnp.sum(weights.reshape(step // 8, 8, cols), axis=0)
            acc = acc + jnp.dot(
                vt_ref[:, starts[n] + at : starts[n] + at + step],
                weights.astype(jnp.bfloat16),
                preferred_element_type=jnp.float32,
            )
    out_ref[0:HD, :] = acc
    out_ref[HD : HD + 8, :] = total
    out_ref[HD + 8 :, :] = jnp.broadcast_to(reference, (8, cols))
    safe = jnp.max(total) < LIMIT

    @pl.when(jnp.logical_not(safe))
    def _():
        if first:
            out_ref[0 : HD + 8, :] = jnp.zeros((HD + 8, cols), jnp.float32)
        else:
            out_ref[...] = in_ref[...]
        for n, kv in enumerate(kv_refs):

            def absorb(i, carry, kv=kv, n=n):
                at = pl.multiple_of(i * 256, 256)
                scores = scores_of(kv[pl.ds(at, 256), :HD])
                old = out_ref[HD + 8 : HD + 9, :]
                new = jnp.maximum(old, jnp.max(scores, axis=0, keepdims=True))
                rescale = jnp.exp2(old - new)
                weights = jnp.exp2(scores - new)
                out_ref[HD : HD + 8, :] = out_ref[HD : HD + 8, :] * rescale + jnp.sum(
                    weights.reshape(32, 8, cols), axis=0
                )
                out_ref[0:HD, :] = out_ref[0:HD, :] * rescale + jnp.dot(
                    vt_ref[:, pl.ds(pl.multiple_of(starts[n] + at, 256), 256)],
                    weights.astype(jnp.bfloat16),
                    preferred_element_type=jnp.float32,
                )
                out_ref[HD + 8 :, :] = jnp.broadcast_to(new, (8, cols))
                return carry

            lax.fori_loop(0, kv.shape[0] // 256, absorb, 0)


def attend(q, kvs, state=None, columns=None, offset=0, fill=None, block=1280):
    rows = q.shape[0]
    first = state is None
    keys = sum(kv.shape[0] for kv in kvs)
    shift = offset // block
    write = shift if columns else 0
    in_specs = [pl.BlockSpec((block, HD), lambda i: (i, 0))]
    in_specs += [pl.BlockSpec(kv.shape, lambda i: (0, 0)) for kv in kvs]
    args = [q] + list(kvs)
    aliases = {}
    if not first:
        in_specs.append(pl.BlockSpec((STATE, block), lambda i: (0, i + shift)))
        args.append(state)
    if fill is not None:
        aliases = {len(args): 0}
        in_specs.append(pl.BlockSpec(memory_space=pl.ANY))
        args.append(fill)
    return pl.pallas_call(
        functools.partial(attention_kernel, pieces=len(kvs), first=first, filled=fill is not None),
        grid=(rows // block,),
        in_specs=in_specs,
        out_specs=pl.BlockSpec((STATE, block), lambda i: (0, i + write)),
        out_shape=jax.ShapeDtypeStruct((STATE, columns or rows), jnp.float32),
        scratch_shapes=[pltpu.VMEM((HD, keys), jnp.bfloat16)],
        input_output_aliases=aliases,
        compiler_params=pltpu.CompilerParams(vmem_limit_bytes=ATTEND_MIB * MIB),
        cost_estimate=pl.CostEstimate(
            flops=rows * keys * 6 * HD,
            bytes_accessed=rows * 1408 + keys * 512,
            transcendentals=rows * keys,
        ),
    )(*args)


def band_selection():
    chosen = np.zeros((BANDS, 8, WIDE, 8 * PW), np.float32)
    for band in range(BANDS):
        for col in range(WIDE):
            place = band * BAND - 1 + col
            if 0 <= place < PW:
                for row in range(8):
                    chosen[band, row, col, row * PW + place] = 1.0
    return chosen.reshape(BANDS * 8 * WIDE, 8 * PW)


def combine_kernel(mine_ref, other_ref, choose_ref, out_ref):
    lanes = 8 * PW
    for group in range(4):
        at = slice(group * lanes, (group + 1) * lanes)
        ref_a, ref_b = (mine_ref[HD + 8 : HD + 9, at], other_ref[HD + 8 : HD + 9, at])
        top = jnp.maximum(ref_a, ref_b)
        gain_a, gain_b = (jnp.exp2(ref_a - top), jnp.exp2(ref_b - top))
        total = jnp.sum(
            mine_ref[HD : HD + 8, at] * gain_a + other_ref[HD : HD + 8, at] * gain_b,
            axis=0,
            keepdims=True,
        )
        attended = (mine_ref[0:HD, at] * gain_a + other_ref[0:HD, at] * gain_b) / total
        banded = dot_nt(choose_ref[...], attended.astype(jnp.bfloat16)).astype(jnp.bfloat16)
        frame, half = divmod(group, 2)
        out_ref[frame * BANDS : (frame + 1) * BANDS, half * 64 : (half + 1) * 64, :] = banded.reshape(
            BANDS, 64, HD
        )


def combine(mine, other):
    choose = jnp.asarray(band_selection(), jnp.bfloat16)
    return pl.pallas_call(
        combine_kernel,
        out_shape=jax.ShapeDtypeStruct((2 * BANDS, 128, HD), jnp.bfloat16),
        compiler_params=pltpu.CompilerParams(vmem_limit_bytes=20 * MIB),
    )(mine, other, choose)


def window_selection():
    chosen = np.zeros((3, 4 * C_LAT, 2, 4, C_LAT), np.float32)
    for i in range(2):
        for col in range(4):
            side, j = divmod(col + 1, 2)
            for ch in range(C_LAT):
                chosen[side, 4 * ch + 2 * i + j, i, col, ch] = 1.0
    return chosen.reshape(3, 4 * C_LAT, 128)


TILE_N = 512


def project_kernel(
    band_ref, x_ref, w_ref, shift_ref, scale_ref, final_ref, choose_ref, out_ref, rows_ref, proj_ref, tiles_ref, sems
):
    tiles = D // TILE_N

    def fetch(n):
        return pltpu.make_async_copy(w_ref.at[:, pl.ds(n * TILE_N, TILE_N)], tiles_ref.at[n], sems.at[n])

    for n in range(tiles):
        fetch(n).start()
    for head in range(HEADS):
        for core in range(2):
            block = x_ref[head, core].reshape(8, 16, HD)
            for pair in range(8):
                at = pair * 32 + core * 16
                rows_ref[at : at + 16, head * HD : (head + 1) * HD] = block[pair]
    total = jnp.zeros((PH * WIDE, 1), jnp.float32)
    for n in range(tiles):
        fetch(n).wait()
        part = jnp.dot(rows_ref[...], tiles_ref[n], preferred_element_type=jnp.float32)
        proj_ref[n] = part
        total = total + jnp.sum(part, axis=1, keepdims=True)
    mean = total / D
    square = 0.0
    for n in range(tiles):
        centered = proj_ref[n] - mean
        square = square + jnp.sum(centered * centered, axis=1, keepdims=True)
    inverse = 1.0 / jnp.sqrt(square / D + 1e-06)
    patches = jnp.zeros((PH * WIDE, 4 * C_LAT), jnp.float32)
    for n in range(tiles):
        at = slice(n * TILE_N, (n + 1) * TILE_N)
        normed = (proj_ref[n] - mean) * inverse * (1.0 + scale_ref[:, at]) + shift_ref[:, at]
        patches = patches + jnp.dot(
            normed.astype(jnp.bfloat16), final_ref[at, :], preferred_element_type=jnp.float32
        )
    patches = patches.astype(jnp.bfloat16).astype(jnp.float32)
    place = lax.rem(lax.broadcasted_iota(jnp.int32, patches.shape, 0), WIDE) + (band_ref[0] * BAND - 1)
    patches = jnp.where((place >= 0) & (place < PW), patches, 0.0)
    wide = jnp.zeros((PH * WIDE, 128), jnp.float32)
    for side in range(3):
        moved = patches if side == 0 else pltpu.roll(patches, PH * WIDE - side, 0)
        wide = wide + jnp.dot(moved.astype(jnp.bfloat16), choose_ref[side], preferred_element_type=jnp.float32)
    out_ref[...] = wide.astype(jnp.bfloat16)


def project(band, gathered, w_out, shift_vec, scale_vec, w_final):
    choose = jnp.asarray(window_selection(), jnp.bfloat16)
    vmem = pl.BlockSpec(memory_space=pltpu.VMEM)
    return pl.pallas_call(
        project_kernel,
        in_specs=[pl.BlockSpec(memory_space=pltpu.SMEM), vmem, pl.BlockSpec(memory_space=pl.ANY)] + [vmem] * 4,
        out_specs=vmem,
        out_shape=jax.ShapeDtypeStruct((PH * WIDE, 128), jnp.bfloat16),
        scratch_shapes=[
            pltpu.VMEM((PH * WIDE, HEADS * HD), jnp.bfloat16),
            pltpu.VMEM((D // TILE_N, PH * WIDE, TILE_N), jnp.float32),
            pltpu.VMEM((D // TILE_N, HEADS * HD, TILE_N), jnp.bfloat16),
            pltpu.SemaphoreType.DMA((D // TILE_N,)),
        ],
        compiler_params=pltpu.CompilerParams(vmem_limit_bytes=52 * MIB),
    )(band, gathered, w_out, shift_vec.reshape(1, D), scale_vec.reshape(1, D), w_final, choose)


def conv_kernel(frame_ref, now_ref, one_ref, two_ref, w_ref, out_ref, taps_ref, grid_ref, spread_ref):
    rows = PH * WIDE
    taps_ref[...] = jnp.zeros_like(taps_ref)
    for odd in range(2):
        for a in range(3):
            for b in range(3):
                y = odd + b - 1
                offset = {-1: 192, 0: 0, 1: 64, 2: 128}[y]
                for j in range(2):
                    for e in range(3):
                        at = offset + (j + e) * C_LAT
                        tap = ((a * 3 + b) * 3 + e) * C_LAT
                        taps_ref[odd, a, at : at + C_LAT, j * C_VAE : (j + 1) * C_VAE] = w_ref[tap : tap + C_LAT, :]
    frame = frame_ref[0]
    now = now_ref[...].astype(jnp.float32)
    one = jnp.where(frame >= 1, one_ref[...].astype(jnp.float32), now)
    two = jnp.where(frame >= 2, two_ref[...].astype(jnp.float32), one)
    gap = jnp.zeros((WIDE, 128), jnp.float32)
    for a, grid in enumerate((two, one, now)):
        grid_ref[a, 0:WIDE, :] = gap
        grid_ref[a, WIDE : WIDE + rows, :] = grid
        grid_ref[a, WIDE + rows :, :] = gap

    def column_major(a, down):
        parts = [grid_ref[a, pl.ds((1 + down) * WIDE + col, PH, stride=WIDE), :] for col in range(BAND)]
        return jnp.concatenate(parts, axis=0).astype(jnp.bfloat16)

    for odd in range(2):
        result = jnp.zeros((BAND * PH, 2 * C_VAE), jnp.float32)
        for a in range(3):
            window = jnp.concatenate([column_major(a, 0), column_major(a, 2 * odd - 1)], axis=1)
            result = result + jnp.dot(window, taps_ref[odd, a], preferred_element_type=jnp.float32)
        for col in range(BAND):
            for j in range(2):
                for part in range(C_VAE // 128):
                    at = j * C_VAE + part * 128
                    spread_ref[part, pl.ds((2 * col + j) * 2 * PH + odd, PH, stride=2), :] = result[
                        col * PH : (col + 1) * PH, at : at + 128
                    ]
    for part in range(C_VAE // 128):
        final = spread_ref[part].reshape(2 * BAND, 2 * PH, 128)
        out_ref[:, :, part * 128 : (part + 1) * 128] = final.astype(jnp.bfloat16)


def convolve(frame, now, one, two, w_conv):
    return pl.pallas_call(
        conv_kernel,
        grid=(1,),
        in_specs=[pl.BlockSpec(memory_space=pltpu.SMEM)]
        + [pl.BlockSpec((PH * WIDE, 128), lambda i: (0, 0))] * 3
        + [pl.BlockSpec((27 * C_LAT, C_VAE), lambda i: (0, 0))],
        out_specs=pl.BlockSpec((2 * BAND, 2 * PH, C_VAE), lambda i: (0, 0, 0)),
        out_shape=jax.ShapeDtypeStruct((2 * BAND, 2 * PH, C_VAE), jnp.bfloat16),
        scratch_shapes=[
            pltpu.VMEM((2, 3, 256, 2 * C_VAE), jnp.bfloat16),
            pltpu.VMEM((3, (PH + 2) * WIDE, 128), jnp.float32),
            pltpu.VMEM((C_VAE // 128, 4 * BAND * PH, 128), jnp.float32),
        ],
        compiler_params=pltpu.CompilerParams(vmem_limit_bytes=24 * MIB),
    )(frame, now, one, two, w_conv.reshape(27 * C_LAT, C_VAE))


def pack_kernel(key_ref, value_ref, query_ref, out_ref):
    for n, ref in enumerate((key_ref, value_ref, query_ref)):
        for head in range(HEADS):
            out_ref[head, :, n * HD : (n + 1) * HD] = ref[:, head * HD : (head + 1) * HD]


def pack(key_rows, value_rows, queries):
    vmem = pl.BlockSpec(memory_space=pltpu.VMEM)
    return pl.pallas_call(
        pack_kernel,
        in_specs=[vmem] * 3,
        out_specs=vmem,
        out_shape=jax.ShapeDtypeStruct((HEADS, queries.shape[0], 3 * HD), jnp.bfloat16),
    )(key_rows, value_rows, queries)


def ring(x, axis, by):
    count = lax.axis_size(axis)
    return lax.ppermute(x, axis, [(i, (i + by) % count) for i in range(count)])


def later(x, by):
    count = lax.axis_size(("y", "zl"))
    return lax.ppermute(x, ("y", "zl"), [(i, i + by) for i in range(count - by)])


def per_device(queries, key_rows, value_rows, w_out, shift_vec, scale_vec, w_final, w_conv):
    tokens = queries.shape[0]

    outgoing = pack(key_rows, value_rows, queries)
    incoming = lax.all_to_all(outgoing, PLANE, 0, 0, tiled=True).reshape(HEADS * tokens, 3 * HD)
    half = HEADS * tokens // 2
    kv = incoming[:, : 2 * HD]
    kv_a, kv_b = (kv[:half], kv[half:])
    q_mine = incoming[:, 2 * HD :]
    below_a, above_b = (ring(kv_a, "y", 1), ring(kv_b, "y", -1))
    q_theirs = ring(q_mine, "c", 1)
    columns = 4 * half
    state = attend(q_mine, [kv_a, kv_b], columns=columns)
    kv_a, kv_b, q_theirs, state = lax.optimization_barrier((kv_a, kv_b, q_theirs, state))
    below_b, above_a = (ring(kv_b, "y", 1), ring(kv_a, "y", -1))
    state = attend(q_theirs, [kv_a, kv_b], columns=columns, offset=2 * half, fill=state)
    q_all = jnp.concatenate([q_mine, q_theirs], axis=0)
    below_a, above_b, state = lax.optimization_barrier((below_a, above_b, state))
    far_a, far_b = (ring(below_a, "y", 1), ring(above_b, "y", -1))
    state = attend(q_all, [below_a, above_b], state)
    below_b, above_a, state = lax.optimization_barrier((below_b, above_a, state))
    state = attend(q_all, [below_b, above_a], state)
    far_a, far_b, state = lax.optimization_barrier((far_a, far_b, state))
    theirs = attend(q_theirs, [far_a, far_b], state, offset=2 * half)
    theirs = ring(theirs, "c", 1)
    mine = attend(q_mine, [far_a, far_b], state)
    banded = combine(mine, theirs)
    gathered = lax.all_to_all(banded, ("zl", "x", "zh", "c"), 0, 0, tiled=True)
    gathered = gathered.reshape(HEADS, 2, 128, HD)
    band = lax.axis_index(("x", "zh", "c")).astype(jnp.int32).reshape(1)
    frame = lax.axis_index(("y", "zl")).astype(jnp.int32).reshape(1)
    now = project(band, gathered, w_out, shift_vec, scale_vec, w_final)
    decoded = convolve(frame, now, later(now, 1), later(now, 2), w_conv)
    return decoded.transpose(1, 0, 2)[None]


def solution(mesh):
    fine = Mesh(mesh.devices.reshape(SIZES), AXES)
    rows = P(AXES, None)
    return jax.shard_map(
        per_device,
        mesh=fine,
        in_specs=(rows, rows, rows, P(), P(), P(), P(), P()),
        out_specs=P(("y", "zl"), None, ("x", "zh", "c"), None),
        check_vma=False,
    )
```

```python
import functools

import jax
import jax.numpy as jnp
import numpy as np
from jax import lax
from jax.experimental import pallas as pl
from jax.experimental.pallas import tpu as pltpu
from jax.sharding import Mesh, PartitionSpec as P

HD = 128
HEADS = 16
D = 3072
C_LAT = 16
C_VAE = 512
PW = 80
PH = 32
BANDS = 16
BAND = 5
WIDE = 8
AXES = ("y", "zl", "x", "zh", "c")
SIZES = (4, 2, 4, 2, 2)
PLANE = ("zl", "x", "zh")
SCALE_LOG2 = HD ** -0.5 * 1.4426950408889634
LIMIT = 1e30
NT = (((1,), (1,)), ((), ()))
STATE = HD + 16
MIB = 2 ** 20
ATTEND_MIB = 36


def dot_nt(a, b):
    return lax.dot_general(a, b, NT, preferred_element_type=jnp.float32)


def attention_kernel(*refs, pieces, first, filled):
    q_ref = refs[0]
    kv_refs = refs[1 : 1 + pieces]
    rest = refs[1 + pieces :]
    if filled:
        rest = rest[1:]
    if first:
        out_ref, keys_ref, vt_ref = rest
    else:
        in_ref, out_ref, keys_ref, vt_ref = rest
    starts = [0]
    for kv in kv_refs:
        starts.append(starts[-1] + kv.shape[0])

    @pl.when(pl.program_id(0) == 0)
    def _():
        for n, kv in enumerate(kv_refs):
            keys_ref[starts[n] : starts[n + 1], :] = kv[:, :HD]
            vt_ref[:, starts[n] : starts[n + 1]] = kv[:, HD:].T

    q_scaled = q_ref[...].astype(jnp.float32) * SCALE_LOG2
    q_hi = q_scaled.astype(jnp.bfloat16)
    q_lo = (q_scaled - q_hi.astype(jnp.float32)).astype(jnp.bfloat16)
    q_pair = jnp.concatenate([q_hi, q_lo], axis=1)
    cols = q_pair.shape[0]

    def scores_of(keys):
        return dot_nt(jnp.concatenate([keys, keys], axis=1), q_pair)

    if first:
        reference = jnp.max(scores_of(kv_refs[0][0:256, :HD]), axis=0, keepdims=True)
        total = jnp.zeros((8, cols), jnp.float32)
        acc = jnp.zeros((HD, cols), jnp.float32)
    else:
        reference = in_ref[HD + 8 : HD + 9, :]
        total = in_ref[HD : HD + 8, :]
        acc = in_ref[0:HD, :]
    for n, kv in enumerate(kv_refs):
        size = kv.shape[0]
        step = min(size, 1280)
        for at in range(0, size, step):
            weights = jnp.exp2(scores_of(kv[at : at + step, :HD]) - reference)
            total = total + jnp.sum(weights.reshape(step // 8, 8, cols), axis=0)
            acc = acc + jnp.dot(
                vt_ref[:, starts[n] + at : starts[n] + at + step],
                weights.astype(jnp.bfloat16),
                preferred_element_type=jnp.float32,
            )
    out_ref[0:HD, :] = acc
    out_ref[HD : HD + 8, :] = total
    out_ref[HD + 8 :, :] = jnp.broadcast_to(reference, (8, cols))
    safe = jnp.max(total) < LIMIT

    @pl.when(jnp.logical_not(safe))
    def _():
        if first:
            out_ref[0 : HD + 8, :] = jnp.zeros((HD + 8, cols), jnp.float32)
        else:
            out_ref[...] = in_ref[...]

        def absorb(i, carry):
            at = pl.multiple_of(i * 128, 128)
            scores = scores_of(keys_ref[pl.ds(at, 128), :])
            old = out_ref[HD + 8 : HD + 9, :]
            new = jnp.maximum(old, jnp.max(scores, axis=0, keepdims=True))
            rescale = jnp.exp2(old - new)
            weights = jnp.exp2(scores - new)
            out_ref[HD : HD + 8, :] = out_ref[HD : HD + 8, :] * rescale + jnp.sum(
                weights.reshape(16, 8, cols), axis=0
            )
            out_ref[0:HD, :] = out_ref[0:HD, :] * rescale + jnp.dot(
                vt_ref[:, pl.ds(at, 128)], weights.astype(jnp.bfloat16), preferred_element_type=jnp.float32
            )
            out_ref[HD + 8 :, :] = jnp.broadcast_to(new, (8, cols))
            return carry

        lax.fori_loop(0, starts[-1] // 128, absorb, 0)


def attend(q, kvs, state=None, columns=None, offset=0, fill=None, block=1280):
    rows = q.shape[0]
    first = state is None
    keys = sum(kv.shape[0] for kv in kvs)
    shift = offset // block
    write = shift if columns else 0
    in_specs = [pl.BlockSpec((block, HD), lambda i: (i, 0))]
    in_specs += [pl.BlockSpec(kv.shape, lambda i: (0, 0)) for kv in kvs]
    args = [q] + list(kvs)
    aliases = {}
    if not first:
        in_specs.append(pl.BlockSpec((STATE, block), lambda i: (0, i + shift)))
        args.append(state)
    if fill is not None:
        aliases = {len(args): 0}
        in_specs.append(pl.BlockSpec(memory_space=pl.ANY))
        args.append(fill)
    return pl.pallas_call(
        functools.partial(attention_kernel, pieces=len(kvs), first=first, filled=fill is not None),
        grid=(rows // block,),
        in_specs=in_specs,
        out_specs=pl.BlockSpec((STATE, block), lambda i: (0, i + write)),
        out_shape=jax.ShapeDtypeStruct((STATE, columns or rows), jnp.float32),
        scratch_shapes=[pltpu.VMEM((keys, HD), jnp.bfloat16), pltpu.VMEM((HD, keys), jnp.bfloat16)],
        input_output_aliases=aliases,
        compiler_params=pltpu.CompilerParams(vmem_limit_bytes=ATTEND_MIB * MIB),
        cost_estimate=pl.CostEstimate(
            flops=rows * keys * 6 * HD,
            bytes_accessed=rows * 1408 + keys * 512,
            transcendentals=rows * keys,
        ),
    )(*args)


def band_selection():
    chosen = np.zeros((BANDS, 8, WIDE, 8 * PW), np.float32)
    for band in range(BANDS):
        for col in range(WIDE):
            place = band * BAND - 1 + col
            if 0 <= place < PW:
                for row in range(8):
                    chosen[band, row, col, row * PW + place] = 1.0
    return chosen.reshape(BANDS * 8 * WIDE, 8 * PW)


def combine_kernel(mine_ref, other_ref, choose_ref, out_ref):
    lanes = 8 * PW
    for group in range(4):
        at = slice(group * lanes, (group + 1) * lanes)
        ref_a, ref_b = (mine_ref[HD + 8 : HD + 9, at], other_ref[HD + 8 : HD + 9, at])
        top = jnp.maximum(ref_a, ref_b)
        gain_a, gain_b = (jnp.exp2(ref_a - top), jnp.exp2(ref_b - top))
        total = jnp.sum(
            mine_ref[HD : HD + 8, at] * gain_a + other_ref[HD : HD + 8, at] * gain_b,
            axis=0,
            keepdims=True,
        )
        attended = (mine_ref[0:HD, at] * gain_a + other_ref[0:HD, at] * gain_b) / total
        banded = dot_nt(choose_ref[...], attended.astype(jnp.bfloat16)).astype(jnp.bfloat16)
        frame, half = divmod(group, 2)
        out_ref[frame * BANDS : (frame + 1) * BANDS, half * 64 : (half + 1) * 64, :] = banded.reshape(
            BANDS, 64, HD
        )


def combine(mine, other):
    choose = jnp.asarray(band_selection(), jnp.bfloat16)
    return pl.pallas_call(
        combine_kernel,
        out_shape=jax.ShapeDtypeStruct((2 * BANDS, 128, HD), jnp.bfloat16),
        compiler_params=pltpu.CompilerParams(vmem_limit_bytes=20 * MIB),
    )(mine, other, choose)


def window_selection():
    chosen = np.zeros((3, 4 * C_LAT, 2, 4, C_LAT), np.float32)
    for i in range(2):
        for col in range(4):
            side, j = divmod(col + 1, 2)
            for ch in range(C_LAT):
                chosen[side, 4 * ch + 2 * i + j, i, col, ch] = 1.0
    return chosen.reshape(3, 4 * C_LAT, 128)


TILE_N = 512


def project_kernel(
    band_ref, x_ref, w_ref, shift_ref, scale_ref, final_ref, choose_ref, out_ref, rows_ref, proj_ref, tiles_ref, sems
):
    tiles = D // TILE_N

    def fetch(n):
        return pltpu.make_async_copy(w_ref.at[:, pl.ds(n * TILE_N, TILE_N)], tiles_ref.at[n], sems.at[n])

    for n in range(tiles):
        fetch(n).start()
    for head in range(HEADS):
        for core in range(2):
            block = x_ref[head, core].reshape(8, 16, HD)
            for pair in range(8):
                at = pair * 32 + core * 16
                rows_ref[at : at + 16, head * HD : (head + 1) * HD] = block[pair]

    def multiply(n, total):
        fetch(n).wait()
        part = jnp.dot(rows_ref[...], tiles_ref[n], preferred_element_type=jnp.float32)
        proj_ref[n] = part
        return total + jnp.sum(part, axis=1, keepdims=True)

    total = jnp.zeros((PH * WIDE, 1), jnp.float32)
    for n in range(tiles):
        total = multiply(n, total)
    mean = total / D

    def measure(n, square):
        centered = proj_ref[n] - mean
        return square + jnp.sum(centered * centered, axis=1, keepdims=True)

    square = lax.fori_loop(0, tiles, measure, jnp.zeros((PH * WIDE, 1), jnp.float32), unroll=2)
    inverse = 1.0 / jnp.sqrt(square / D + 1e-06)

    def reduce(n, patches):
        at = pl.ds(pl.multiple_of(n * TILE_N, TILE_N), TILE_N)
        normed = (proj_ref[n] - mean) * inverse * (1.0 + scale_ref[:, at]) + shift_ref[:, at]
        return patches + jnp.dot(normed.astype(jnp.bfloat16), final_ref[at, :], preferred_element_type=jnp.float32)

    patches = lax.fori_loop(0, tiles, reduce, jnp.zeros((PH * WIDE, 4 * C_LAT), jnp.float32), unroll=2)
    patches = patches.astype(jnp.bfloat16).astype(jnp.float32)
    place = lax.rem(lax.broadcasted_iota(jnp.int32, patches.shape, 0), WIDE) + (band_ref[0] * BAND - 1)
    patches = jnp.where((place >= 0) & (place < PW), patches, 0.0)
    wide = jnp.zeros((PH * WIDE, 128), jnp.float32)
    for side in range(3):
        moved = patches if side == 0 else pltpu.roll(patches, PH * WIDE - side, 0)
        wide = wide + jnp.dot(moved.astype(jnp.bfloat16), choose_ref[side], preferred_element_type=jnp.float32)
    out_ref[...] = wide.astype(jnp.bfloat16)


def project(band, gathered, w_out, shift_vec, scale_vec, w_final):
    choose = jnp.asarray(window_selection(), jnp.bfloat16)
    vmem = pl.BlockSpec(memory_space=pltpu.VMEM)
    return pl.pallas_call(
        project_kernel,
        in_specs=[pl.BlockSpec(memory_space=pltpu.SMEM), vmem, pl.BlockSpec(memory_space=pl.ANY)] + [vmem] * 4,
        out_specs=vmem,
        out_shape=jax.ShapeDtypeStruct((PH * WIDE, 128), jnp.bfloat16),
        scratch_shapes=[
            pltpu.VMEM((PH * WIDE, HEADS * HD), jnp.bfloat16),
            pltpu.VMEM((D // TILE_N, PH * WIDE, TILE_N), jnp.float32),
            pltpu.VMEM((D // TILE_N, HEADS * HD, TILE_N), jnp.bfloat16),
            pltpu.SemaphoreType.DMA((D // TILE_N,)),
        ],
        compiler_params=pltpu.CompilerParams(vmem_limit_bytes=52 * MIB),
    )(band, gathered, w_out, shift_vec.reshape(1, D), scale_vec.reshape(1, D), w_final, choose)


def conv_kernel(frame_ref, now_ref, one_ref, two_ref, w_ref, out_ref, taps_ref, grid_ref, spread_ref):
    rows = PH * WIDE
    taps_ref[...] = jnp.zeros_like(taps_ref)
    for odd in range(2):
        for a in range(3):
            for b in range(3):
                y = odd + b - 1
                offset = {-1: 192, 0: 0, 1: 64, 2: 128}[y]
                for j in range(2):
                    for e in range(3):
                        at = offset + (j + e) * C_LAT
                        tap = ((a * 3 + b) * 3 + e) * C_LAT
                        taps_ref[odd, a, at : at + C_LAT, j * C_VAE : (j + 1) * C_VAE] = w_ref[tap : tap + C_LAT, :]
    frame = frame_ref[0]
    now = now_ref[...].astype(jnp.float32)
    one = jnp.where(frame >= 1, one_ref[...].astype(jnp.float32), now)
    two = jnp.where(frame >= 2, two_ref[...].astype(jnp.float32), one)
    gap = jnp.zeros((WIDE, 128), jnp.float32)
    for a, grid in enumerate((two, one, now)):
        grid_ref[a, 0:WIDE, :] = gap
        grid_ref[a, WIDE : WIDE + rows, :] = grid
        grid_ref[a, WIDE + rows :, :] = gap

    def column_major(a, down):
        parts = [grid_ref[a, pl.ds((1 + down) * WIDE + col, PH, stride=WIDE), :] for col in range(BAND)]
        return jnp.concatenate(parts, axis=0).astype(jnp.bfloat16)

    for odd in range(2):
        result = jnp.zeros((BAND * PH, 2 * C_VAE), jnp.float32)
        for a in range(3):
            window = jnp.concatenate([column_major(a, 0), column_major(a, 2 * odd - 1)], axis=1)
            result = result + jnp.dot(window, taps_ref[odd, a], preferred_element_type=jnp.float32)
        for col in range(BAND):
            for j in range(2):
                for part in range(C_VAE // 128):
                    at = j * C_VAE + part * 128
                    spread_ref[part, pl.ds((2 * col + j) * 2 * PH + odd, PH, stride=2), :] = result[
                        col * PH : (col + 1) * PH, at : at + 128
                    ]
    for part in range(C_VAE // 128):
        final = spread_ref[part].reshape(2 * BAND, 2 * PH, 128)
        out_ref[:, :, part * 128 : (part + 1) * 128] = final.astype(jnp.bfloat16)


def convolve(frame, now, one, two, w_conv):
    return pl.pallas_call(
        conv_kernel,
        grid=(1,),
        in_specs=[pl.BlockSpec(memory_space=pltpu.SMEM)]
        + [pl.BlockSpec((PH * WIDE, 128), lambda i: (0, 0))] * 3
        + [pl.BlockSpec((27 * C_LAT, C_VAE), lambda i: (0, 0))],
        out_specs=pl.BlockSpec((2 * BAND, 2 * PH, C_VAE), lambda i: (0, 0, 0)),
        out_shape=jax.ShapeDtypeStruct((2 * BAND, 2 * PH, C_VAE), jnp.bfloat16),
        scratch_shapes=[
            pltpu.VMEM((2, 3, 256, 2 * C_VAE), jnp.bfloat16),
            pltpu.VMEM((3, (PH + 2) * WIDE, 128), jnp.float32),
            pltpu.VMEM((C_VAE // 128, 4 * BAND * PH, 128), jnp.float32),
        ],
        compiler_params=pltpu.CompilerParams(vmem_limit_bytes=24 * MIB),
    )(frame, now, one, two, w_conv.reshape(27 * C_LAT, C_VAE))


def ring(x, axis, by):
    count = lax.axis_size(axis)
    return lax.ppermute(x, axis, [(i, (i + by) % count) for i in range(count)])


def later(x, by):
    count = lax.axis_size(("y", "zl"))
    return lax.ppermute(x, ("y", "zl"), [(i, i + by) for i in range(count - by)])


def per_device(queries, key_rows, value_rows, w_out, shift_vec, scale_vec, w_final, w_conv):
    tokens = queries.shape[0]

    def by_head(x):
        return x.reshape(tokens, HEADS, HD).transpose(1, 0, 2)

    outgoing = jnp.concatenate([by_head(key_rows), by_head(value_rows), by_head(queries)], axis=2)
    incoming = lax.all_to_all(outgoing, PLANE, 0, 0, tiled=True).reshape(HEADS * tokens, 3 * HD)
    half = HEADS * tokens // 2
    kv = incoming[:, : 2 * HD]
    kv_a, kv_b = (kv[:half], kv[half:])
    q_mine = incoming[:, 2 * HD :]
    below_a, above_b = (ring(kv_a, "y", 1), ring(kv_b, "y", -1))
    q_theirs = ring(q_mine, "c", 1)
    columns = 4 * half
    state = attend(q_mine, [kv_a, kv_b], columns=columns)
    kv_a, kv_b, q_theirs, state = lax.optimization_barrier((kv_a, kv_b, q_theirs, state))
    below_b, above_a = (ring(kv_b, "y", 1), ring(kv_a, "y", -1))
    state = attend(q_theirs, [kv_a, kv_b], columns=columns, offset=2 * half, fill=state)
    q_all = jnp.concatenate([q_mine, q_theirs], axis=0)
    below_a, above_b, state = lax.optimization_barrier((below_a, above_b, state))
    far_a, far_b = (ring(below_a, "y", 1), ring(above_b, "y", -1))
    state = attend(q_all, [below_a, above_b], state)
    below_b, above_a, state = lax.optimization_barrier((below_b, above_a, state))
    state = attend(q_all, [below_b, above_a], state)
    far_a, far_b, state = lax.optimization_barrier((far_a, far_b, state))
    theirs = attend(q_theirs, [far_a, far_b], state, offset=2 * half)
    theirs = ring(theirs, "c", 1)
    mine = attend(q_mine, [far_a, far_b], state)
    banded = combine(mine, theirs)
    gathered = lax.all_to_all(banded, ("zl", "x", "zh", "c"), 0, 0, tiled=True)
    gathered = gathered.reshape(HEADS, 2, 128, HD)
    band = lax.axis_index(("x", "zh", "c")).astype(jnp.int32).reshape(1)
    frame = lax.axis_index(("y", "zl")).astype(jnp.int32).reshape(1)
    now = project(band, gathered, w_out, shift_vec, scale_vec, w_final)
    decoded = convolve(frame, now, later(now, 1), later(now, 2), w_conv)
    return decoded.transpose(1, 0, 2)[None]


def solution(mesh):
    fine = Mesh(mesh.devices.reshape(SIZES), AXES)
    rows = P(AXES, None)
    return jax.shard_map(
        per_device,
        mesh=fine,
        in_specs=(rows, rows, rows, P(), P(), P(), P(), P()),
        out_specs=P(("y", "zl"), None, ("x", "zh", "c"), None),
        check_vma=False,
    )
```

```python
import functools

import jax
import jax.numpy as jnp
import numpy as np
from jax import lax
from jax.experimental import pallas as pl
from jax.experimental.pallas import tpu as pltpu
from jax.sharding import Mesh, PartitionSpec as P

HD = 128
HEADS = 16
D = 3072
C_LAT = 16
C_VAE = 512
PW = 80
PH = 32
BANDS = 16
BAND = 5
WIDE = 7
ROWS = 8 * PW
AXES = ("y", "zl", "x", "zh", "c")
SIZES = (4, 2, 4, 2, 2)
PLANE = ("zl", "x", "zh")
SCALE_LOG2 = HD ** -0.5 * 1.4426950408889634
LIMIT = 1e30
NT = (((1,), (1,)), ((), ()))
STATE = HD + 16
MIB = 2 ** 20
ATTEND_MIB = 36


def dot_nt(a, b):
    return lax.dot_general(a, b, NT, preferred_element_type=jnp.float32)


def attention_kernel(*refs, pieces, first, filled):
    q_ref = refs[0]
    kv_refs = refs[1 : 1 + pieces]
    rest = refs[1 + pieces :]
    if filled:
        rest = rest[1:]
    if first:
        out_ref, keys_ref, vt_ref = rest
    else:
        in_ref, out_ref, keys_ref, vt_ref = rest
    starts = [0]
    for kv in kv_refs:
        starts.append(starts[-1] + kv.shape[0])

    @pl.when(pl.program_id(0) == 0)
    def _():
        for n, kv in enumerate(kv_refs):
            keys_ref[starts[n] : starts[n + 1], :] = kv[:, :HD]
            vt_ref[:, starts[n] : starts[n + 1]] = kv[:, HD:].T

    q_scaled = q_ref[...].astype(jnp.float32) * SCALE_LOG2
    q_hi = q_scaled.astype(jnp.bfloat16)
    q_lo = (q_scaled - q_hi.astype(jnp.float32)).astype(jnp.bfloat16)
    q_pair = jnp.concatenate([q_hi, q_lo], axis=1)
    cols = q_pair.shape[0]

    def scores_of(keys):
        return dot_nt(jnp.concatenate([keys, keys], axis=1), q_pair)

    if first:
        reference = jnp.max(scores_of(kv_refs[0][0:256, :HD]), axis=0, keepdims=True)
        total = jnp.zeros((8, cols), jnp.float32)
        acc = jnp.zeros((HD, cols), jnp.float32)
    else:
        reference = in_ref[HD + 8 : HD + 9, :]
        total = in_ref[HD : HD + 8, :]
        acc = in_ref[0:HD, :]
    for n, kv in enumerate(kv_refs):
        size = kv.shape[0]
        step = min(size, 1280)
        for at in range(0, size, step):
            weights = jnp.exp2(scores_of(kv[at : at + step, :HD]) - reference)
            total = total + jnp.sum(weights.reshape(step // 8, 8, cols), axis=0)
            acc = acc + jnp.dot(
                vt_ref[:, starts[n] + at : starts[n] + at + step],
                weights.astype(jnp.bfloat16),
                preferred_element_type=jnp.float32,
            )
    out_ref[0:HD, :] = acc
    out_ref[HD : HD + 8, :] = total
    out_ref[HD + 8 :, :] = jnp.broadcast_to(reference, (8, cols))
    safe = jnp.max(total) < LIMIT

    @pl.when(jnp.logical_not(safe))
    def _():
        if first:
            out_ref[0 : HD + 8, :] = jnp.zeros((HD + 8, cols), jnp.float32)
        else:
            out_ref[...] = in_ref[...]

        def absorb(i, carry):
            at = pl.multiple_of(i * 128, 128)
            scores = scores_of(keys_ref[pl.ds(at, 128), :])
            old = out_ref[HD + 8 : HD + 9, :]
            new = jnp.maximum(old, jnp.max(scores, axis=0, keepdims=True))
            rescale = jnp.exp2(old - new)
            weights = jnp.exp2(scores - new)
            out_ref[HD : HD + 8, :] = out_ref[HD : HD + 8, :] * rescale + jnp.sum(
                weights.reshape(16, 8, cols), axis=0
            )
            out_ref[0:HD, :] = out_ref[0:HD, :] * rescale + jnp.dot(
                vt_ref[:, pl.ds(at, 128)], weights.astype(jnp.bfloat16), preferred_element_type=jnp.float32
            )
            out_ref[HD + 8 :, :] = jnp.broadcast_to(new, (8, cols))
            return carry

        lax.fori_loop(0, starts[-1] // 128, absorb, 0)


def attend(q, kvs, state=None, columns=None, offset=0, fill=None, block=1280):
    rows = q.shape[0]
    first = state is None
    keys = sum(kv.shape[0] for kv in kvs)
    shift = offset // block
    write = shift if columns else 0
    in_specs = [pl.BlockSpec((block, HD), lambda i: (i, 0))]
    in_specs += [pl.BlockSpec(kv.shape, lambda i: (0, 0)) for kv in kvs]
    args = [q] + list(kvs)
    aliases = {}
    if not first:
        in_specs.append(pl.BlockSpec((STATE, block), lambda i: (0, i + shift)))
        args.append(state)
    if fill is not None:
        aliases = {len(args): 0}
        in_specs.append(pl.BlockSpec(memory_space=pl.ANY))
        args.append(fill)
    return pl.pallas_call(
        functools.partial(attention_kernel, pieces=len(kvs), first=first, filled=fill is not None),
        grid=(rows // block,),
        in_specs=in_specs,
        out_specs=pl.BlockSpec((STATE, block), lambda i: (0, i + write)),
        out_shape=jax.ShapeDtypeStruct((STATE, columns or rows), jnp.float32),
        scratch_shapes=[pltpu.VMEM((keys, HD), jnp.bfloat16), pltpu.VMEM((HD, keys), jnp.bfloat16)],
        input_output_aliases=aliases,
        compiler_params=pltpu.CompilerParams(vmem_limit_bytes=ATTEND_MIB * MIB),
        cost_estimate=pl.CostEstimate(
            flops=rows * keys * 6 * HD,
            bytes_accessed=rows * 1408 + keys * 512,
            transcendentals=rows * keys,
        ),
    )(*args)


def band_selection():
    chosen = np.zeros((BANDS, WIDE, 8, ROWS), np.float32)
    for band in range(BANDS):
        for col in range(WIDE):
            place = band * BAND - 1 + col
            if 0 <= place < PW:
                for row in range(8):
                    chosen[band, col, row, row * PW + place] = 1.0
    return chosen.reshape(BANDS * WIDE * 8, ROWS)


def combine_kernel(mine_ref, other_ref, choose_ref, out_ref):
    for frame in range(2):
        halves = []
        for half in range(2):
            at = slice((2 * frame + half) * ROWS, (2 * frame + half + 1) * ROWS)
            ref_a, ref_b = (mine_ref[HD + 8 : HD + 9, at], other_ref[HD + 8 : HD + 9, at])
            top = jnp.maximum(ref_a, ref_b)
            gain_a, gain_b = (jnp.exp2(ref_a - top), jnp.exp2(ref_b - top))
            total = jnp.sum(
                mine_ref[HD : HD + 8, at] * gain_a + other_ref[HD : HD + 8, at] * gain_b,
                axis=0,
                keepdims=True,
            )
            attended = (mine_ref[0:HD, at] * gain_a + other_ref[0:HD, at] * gain_b) / total
            halves.append(attended.astype(jnp.bfloat16))
        banded = dot_nt(choose_ref[...], jnp.concatenate(halves, axis=0))
        upper, lower = (banded[:, n * HD : (n + 1) * HD].reshape(BANDS, WIDE, 8, HD) for n in range(2))
        rows = jnp.concatenate([upper, lower], axis=2).astype(jnp.bfloat16)
        out_ref[frame * BANDS : (frame + 1) * BANDS] = rows.reshape(BANDS, WIDE * 16, HD)


def combine(mine, other):
    choose = jnp.asarray(band_selection(), jnp.bfloat16)
    return pl.pallas_call(
        combine_kernel,
        out_shape=jax.ShapeDtypeStruct((2 * BANDS, WIDE * 16, HD), jnp.bfloat16),
        compiler_params=pltpu.CompilerParams(vmem_limit_bytes=20 * MIB),
    )(mine, other, choose)


def window_selection():
    chosen = np.zeros((3, 4 * C_LAT, 2, 4, C_LAT), np.float32)
    for i in range(2):
        for col in range(4):
            side, j = divmod(col + 1, 2)
            for ch in range(C_LAT):
                chosen[side, 4 * ch + 2 * i + j, i, col, ch] = 1.0
    return chosen.reshape(3, 4 * C_LAT, 128)


def row_order():
    chosen = np.zeros((BAND, PH, BAND, PH), np.float32)
    for col in range(BAND):
        for row in range(PH):
            pair, core, low = (row // 4, row // 2 % 2, row % 2)
            chosen[col, row, col, core * 16 + pair * 2 + low] = 1.0
    return chosen.reshape(BAND * PH, BAND * PH)


TILE_N = 512


def project_kernel(
    band_ref, x_ref, w_ref, shift_ref, scale_ref, final_ref, choose_ref, order_ref, out_ref, rows_ref, proj_ref, tiles_ref, sems
):
    tiles = D // TILE_N

    def fetch(n):
        return pltpu.make_async_copy(w_ref.at[:, pl.ds(n * TILE_N, TILE_N)], tiles_ref.at[n], sems.at[n])

    for n in range(tiles):
        fetch(n).start()
    for head in range(HEADS):
        for core in range(2):
            for col in range(WIDE):
                at = col * PH + core * 16
                rows_ref[at : at + 16, head * HD : (head + 1) * HD] = x_ref[head, core, col * 16 : (col + 1) * 16, :]
    total = 0.0
    square = 0.0
    for n in range(tiles):
        fetch(n).wait()
        part = jnp.dot(rows_ref[...], tiles_ref[n], preferred_element_type=jnp.float32)
        proj_ref[n] = part
        part_sum = jnp.sum(part, axis=1, keepdims=True)
        if n == 0:
            near = part_sum / TILE_N
        total = total + part_sum
        square = square + jnp.sum((part - near) * (part - near), axis=1, keepdims=True)
    mean = total / D
    variance = square / D - (mean - near) * (mean - near)
    inverse = 1.0 / jnp.sqrt(variance + 1e-06)

    def reduce(n, patches):
        at = pl.ds(pl.multiple_of(n * TILE_N, TILE_N), TILE_N)
        normed = (proj_ref[n] - mean) * inverse * (1.0 + scale_ref[:, at]) + shift_ref[:, at]
        return patches + jnp.dot(normed.astype(jnp.bfloat16), final_ref[at, :], preferred_element_type=jnp.float32)

    patches = lax.fori_loop(0, tiles, reduce, jnp.zeros((PH * WIDE, 4 * C_LAT), jnp.float32), unroll=2)
    place = lax.broadcasted_iota(jnp.int32, patches.shape, 0) // PH + (band_ref[0] * BAND - 1)
    patches = jnp.where((place >= 0) & (place < PW), patches, 0.0).astype(jnp.bfloat16)
    wide = 0.0
    for side in range(3):
        moved = patches[side * PH : (side + BAND) * PH]
        wide = wide + jnp.dot(moved, choose_ref[side], preferred_element_type=jnp.float32)
    wide = jnp.dot(order_ref[...], wide.astype(jnp.bfloat16), preferred_element_type=jnp.float32)
    out_ref[...] = wide.astype(jnp.bfloat16)


def project(band, gathered, w_out, shift_vec, scale_vec, w_final):
    choose = jnp.asarray(window_selection(), jnp.bfloat16)
    order = jnp.asarray(row_order(), jnp.bfloat16)
    vmem = pl.BlockSpec(memory_space=pltpu.VMEM)
    return pl.pallas_call(
        project_kernel,
        in_specs=[pl.BlockSpec(memory_space=pltpu.SMEM), vmem, pl.BlockSpec(memory_space=pl.ANY)] + [vmem] * 5,
        out_specs=vmem,
        out_shape=jax.ShapeDtypeStruct((BAND * PH, 128), jnp.bfloat16),
        scratch_shapes=[
            pltpu.VMEM((PH * WIDE, HEADS * HD), jnp.bfloat16),
            pltpu.VMEM((D // TILE_N, PH * WIDE, TILE_N), jnp.float32),
            pltpu.VMEM((D // TILE_N, HEADS * HD, TILE_N), jnp.bfloat16),
            pltpu.SemaphoreType.DMA((D // TILE_N,)),
        ],
        compiler_params=pltpu.CompilerParams(vmem_limit_bytes=52 * MIB),
    )(band, gathered, w_out, shift_vec.reshape(1, D), scale_vec.reshape(1, D), w_final, choose, order)


def conv_kernel(frame_ref, now_ref, one_ref, two_ref, w_ref, out_ref, taps_ref, spread_ref):
    rows = BAND * PH
    taps_ref[...] = jnp.zeros_like(taps_ref)
    for odd in range(2):
        for a in range(3):
            for b in range(3):
                y = odd + b - 1
                offset = {-1: 192, 0: 0, 1: 64, 2: 128}[y]
                for j in range(2):
                    for e in range(3):
                        at = offset + (j + e) * C_LAT
                        tap = ((a * 3 + b) * 3 + e) * C_LAT
                        taps_ref[odd, a, at : at + C_LAT, j * C_VAE : (j + 1) * C_VAE] = w_ref[tap : tap + C_LAT, :]
    frame = frame_ref[0]
    now = now_ref[...].astype(jnp.float32)
    one = jnp.where(frame >= 1, one_ref[...].astype(jnp.float32), now)
    two = jnp.where(frame >= 2, two_ref[...].astype(jnp.float32), one)
    row = lax.rem(lax.broadcasted_iota(jnp.int32, (rows, 128), 0), PH)
    for odd in range(2):
        result = jnp.zeros((rows, 2 * C_VAE), jnp.float32)
        for a, grid in enumerate((two, one, now)):
            if odd == 0:
                beside = jnp.where(row == 0, 0.0, pltpu.roll(grid, 1, 0))
            else:
                beside = jnp.where(row == PH - 1, 0.0, pltpu.roll(grid, rows - 1, 0))
            window = jnp.concatenate([grid, beside], axis=1).astype(jnp.bfloat16)
            result = result + jnp.dot(window, taps_ref[odd, a], preferred_element_type=jnp.float32)
        for col in range(BAND):
            for j in range(2):
                for part in range(C_VAE // 128):
                    at = j * C_VAE + part * 128
                    spread_ref[part, pl.ds((2 * col + j) * 2 * PH + odd, PH, stride=2), :] = result[
                        col * PH : (col + 1) * PH, at : at + 128
                    ]
    for part in range(C_VAE // 128):
        final = spread_ref[part].reshape(2 * BAND, 2 * PH, 128)
        out_ref[:, :, part * 128 : (part + 1) * 128] = final.astype(jnp.bfloat16)


def convolve(frame, now, one, two, w_conv):
    return pl.pallas_call(
        conv_kernel,
        grid=(1,),
        in_specs=[pl.BlockSpec(memory_space=pltpu.SMEM)]
        + [pl.BlockSpec((BAND * PH, 128), lambda i: (0, 0))] * 3
        + [pl.BlockSpec((27 * C_LAT, C_VAE), lambda i: (0, 0))],
        out_specs=pl.BlockSpec((2 * BAND, 2 * PH, C_VAE), lambda i: (0, 0, 0)),
        out_shape=jax.ShapeDtypeStruct((2 * BAND, 2 * PH, C_VAE), jnp.bfloat16),
        scratch_shapes=[
            pltpu.VMEM((2, 3, 256, 2 * C_VAE), jnp.bfloat16),
            pltpu.VMEM((C_VAE // 128, 4 * BAND * PH, 128), jnp.float32),
        ],
        compiler_params=pltpu.CompilerParams(vmem_limit_bytes=24 * MIB),
    )(frame, now, one, two, w_conv.reshape(27 * C_LAT, C_VAE))


def ring(x, axis, by):
    count = lax.axis_size(axis)
    return lax.ppermute(x, axis, [(i, (i + by) % count) for i in range(count)])


def later(x, by):
    count = lax.axis_size(("y", "zl"))
    return lax.ppermute(x, ("y", "zl"), [(i, i + by) for i in range(count - by)])


def per_device(queries, key_rows, value_rows, w_out, shift_vec, scale_vec, w_final, w_conv):
    tokens = queries.shape[0]

    def by_head(x):
        return x.reshape(tokens, HEADS, HD).transpose(1, 0, 2)

    outgoing = jnp.concatenate([by_head(key_rows), by_head(value_rows), by_head(queries)], axis=2)
    incoming = lax.all_to_all(outgoing, PLANE, 0, 0, tiled=True).reshape(HEADS * tokens, 3 * HD)
    half = HEADS * tokens // 2
    kv = incoming[:, : 2 * HD]
    kv_a, kv_b = (kv[:half], kv[half:])
    q_mine = incoming[:, 2 * HD :]
    below_a, above_b = (ring(kv_a, "y", 1), ring(kv_b, "y", -1))
    q_theirs = ring(q_mine, "c", 1)
    columns = 4 * half
    state = attend(q_mine, [kv_a, kv_b], columns=columns)
    kv_a, kv_b, q_theirs, state = lax.optimization_barrier((kv_a, kv_b, q_theirs, state))
    below_b, above_a = (ring(kv_b, "y", 1), ring(kv_a, "y", -1))
    state = attend(q_theirs, [kv_a, kv_b], columns=columns, offset=2 * half, fill=state)
    q_all = jnp.concatenate([q_mine, q_theirs], axis=0)
    below_a, above_b, state = lax.optimization_barrier((below_a, above_b, state))
    far_a, far_b = (ring(below_a, "y", 1), ring(above_b, "y", -1))
    state = attend(q_all, [below_a, above_b], state)
    below_b, above_a, state = lax.optimization_barrier((below_b, above_a, state))
    state = attend(q_all, [below_b, above_a], state)
    far_a, far_b, state = lax.optimization_barrier((far_a, far_b, state))
    theirs = attend(q_theirs, [far_a, far_b], state, offset=2 * half)
    theirs = ring(theirs, "c", 1)
    mine = attend(q_mine, [far_a, far_b], state)
    banded = combine(mine, theirs)
    gathered = lax.all_to_all(banded, ("zl", "x", "zh", "c"), 0, 0, tiled=True)
    gathered = gathered.reshape(HEADS, 2, WIDE * 16, HD)
    band = lax.axis_index(("x", "zh", "c")).astype(jnp.int32).reshape(1)
    frame = lax.axis_index(("y", "zl")).astype(jnp.int32).reshape(1)
    now = project(band, gathered, w_out, shift_vec, scale_vec, w_final)
    decoded = convolve(frame, now, later(now, 1), later(now, 2), w_conv)
    return decoded.transpose(1, 0, 2)[None]


def solution(mesh):
    fine = Mesh(mesh.devices.reshape(SIZES), AXES)
    rows = P(AXES, None)
    return jax.shard_map(
        per_device,
        mesh=fine,
        in_specs=(rows, rows, rows, P(), P(), P(), P(), P()),
        out_specs=P(("y", "zl"), None, ("x", "zh", "c"), None),
        check_vma=False,
    )
```

```python
import functools

import jax
import jax.numpy as jnp
import numpy as np
from jax import lax
from jax.experimental import pallas as pl
from jax.experimental.pallas import tpu as pltpu
from jax.sharding import Mesh, PartitionSpec as P

HD = 128
HEADS = 16
D = 3072
C_LAT = 16
C_VAE = 512
PW = 80
PH = 32
BANDS = 16
BAND = 5
WIDE = 7
ROWS = 8 * PW
AXES = ("y", "zl", "x", "zh", "c")
SIZES = (4, 2, 4, 2, 2)
PLANE = ("zl", "x", "zh")
SCALE_LOG2 = HD ** -0.5 * 1.4426950408889634
LIMIT = 1e30
NT = (((1,), (1,)), ((), ()))
STATE = HD + 16
MIB = 2 ** 20
ATTEND_MIB = 36


def dot_nt(a, b):
    return lax.dot_general(a, b, NT, preferred_element_type=jnp.float32)


def attention_kernel(*refs, pieces, first, filled, block, read, write):
    here = pl.multiple_of(pl.program_id(0) * block, block)
    q_ref = refs[0].at[pl.ds(here, block)]
    kv_refs = refs[1 : 1 + pieces]
    rest = refs[1 + pieces :]
    if filled:
        rest = rest[1:]
    if first:
        out_ref, keys_ref, vt_ref = rest
    else:
        in_ref, out_ref, keys_ref, vt_ref = rest
        in_ref = in_ref.at[:, pl.ds(pl.multiple_of(read + here, block), block)]
    out_ref = out_ref.at[:, pl.ds(pl.multiple_of(write + here, block), block)]
    starts = [0]
    for kv in kv_refs:
        starts.append(starts[-1] + kv.shape[0])

    q_scaled = q_ref[...].astype(jnp.float32) * SCALE_LOG2
    q_hi = q_scaled.astype(jnp.bfloat16)
    q_lo = (q_scaled - q_hi.astype(jnp.float32)).astype(jnp.bfloat16)
    q_pair = jnp.concatenate([q_hi, q_lo], axis=1)
    cols = q_pair.shape[0]

    def scores_of(keys):
        return dot_nt(jnp.concatenate([keys, keys], axis=1), q_pair)

    if first:
        reference = jnp.max(scores_of(kv_refs[0][0:256, :HD]), axis=0, keepdims=True)
        total = jnp.zeros((8, cols), jnp.float32)
        acc = jnp.zeros((HD, cols), jnp.float32)
    else:
        reference = in_ref[HD + 8 : HD + 9, :]
        total = in_ref[HD : HD + 8, :]
        acc = in_ref[0:HD, :]
    for n, kv in enumerate(kv_refs):
        size = kv.shape[0]
        step = min(size, 1280)
        for at in range(0, size, step):
            weights = jnp.exp2(scores_of(kv[at : at + step, :HD]) - reference)
            total = total + jnp.sum(weights.reshape(step // 8, 8, cols), axis=0)
            acc = acc + jnp.dot(
                kv[at : at + step, HD:].T,
                weights.astype(jnp.bfloat16),
                preferred_element_type=jnp.float32,
            )
    out_ref[0:HD, :] = acc
    out_ref[HD : HD + 8, :] = total
    out_ref[HD + 8 :, :] = jnp.broadcast_to(reference, (8, cols))
    safe = jnp.max(total) < LIMIT

    @pl.when(jnp.logical_not(safe))
    def _():
        if first:
            out_ref[0 : HD + 8, :] = jnp.zeros((HD + 8, cols), jnp.float32)
        else:
            out_ref[...] = in_ref[...]
        for n, kv in enumerate(kv_refs):
            keys_ref[starts[n] : starts[n + 1], :] = kv[:, :HD]
            vt_ref[:, starts[n] : starts[n + 1]] = kv[:, HD:].T

        def absorb(i, carry):
            at = pl.multiple_of(i * 128, 128)
            scores = scores_of(keys_ref[pl.ds(at, 128), :])
            old = out_ref[HD + 8 : HD + 9, :]
            new = jnp.maximum(old, jnp.max(scores, axis=0, keepdims=True))
            rescale = jnp.exp2(old - new)
            weights = jnp.exp2(scores - new)
            out_ref[HD : HD + 8, :] = out_ref[HD : HD + 8, :] * rescale + jnp.sum(
                weights.reshape(16, 8, cols), axis=0
            )
            out_ref[0:HD, :] = out_ref[0:HD, :] * rescale + jnp.dot(
                vt_ref[:, pl.ds(at, 128)], weights.astype(jnp.bfloat16), preferred_element_type=jnp.float32
            )
            out_ref[HD + 8 :, :] = jnp.broadcast_to(new, (8, cols))
            return carry

        lax.fori_loop(0, starts[-1] // 128, absorb, 0)


def attend(q, kvs, state=None, columns=None, offset=0, fill=None, block=1280):
    rows = q.shape[0]
    first = state is None
    keys = sum(kv.shape[0] for kv in kvs)
    shift = offset // block
    write = shift if columns else 0
    vmem = pl.BlockSpec(memory_space=pltpu.VMEM)
    args = [q] + list(kvs)
    aliases = {}
    if not first:
        args.append(state)
    if fill is not None:
        aliases = {len(args): 0}
        args.append(fill)
    return pl.pallas_call(
        functools.partial(
            attention_kernel,
            pieces=len(kvs),
            first=first,
            filled=fill is not None,
            block=block,
            read=shift * block,
            write=write * block,
        ),
        grid=(rows // block,),
        in_specs=[vmem] * len(args),
        out_specs=vmem,
        out_shape=jax.ShapeDtypeStruct((STATE, columns or rows), jnp.float32),
        scratch_shapes=[pltpu.VMEM((keys, HD), jnp.bfloat16), pltpu.VMEM((HD, keys), jnp.bfloat16)],
        input_output_aliases=aliases,
        compiler_params=pltpu.CompilerParams(vmem_limit_bytes=ATTEND_MIB * MIB),
        cost_estimate=pl.CostEstimate(
            flops=rows * keys * 6 * HD,
            bytes_accessed=rows * 1408 + keys * 512,
            transcendentals=rows * keys,
        ),
    )(*args)


def band_selection():
    chosen = np.zeros((BANDS, WIDE, 8, ROWS), np.float32)
    for band in range(BANDS):
        for col in range(WIDE):
            place = band * BAND - 1 + col
            if 0 <= place < PW:
                for row in range(8):
                    chosen[band, col, row, row * PW + place] = 1.0
    return chosen.reshape(BANDS * WIDE * 8, ROWS)


def combine_kernel(mine_ref, other_ref, choose_ref, out_ref):
    for frame in range(2):
        halves = []
        for half in range(2):
            at = slice((2 * frame + half) * ROWS, (2 * frame + half + 1) * ROWS)
            ref_a, ref_b = (mine_ref[HD + 8 : HD + 9, at], other_ref[HD + 8 : HD + 9, at])
            top = jnp.maximum(ref_a, ref_b)
            gain_a, gain_b = (jnp.exp2(ref_a - top), jnp.exp2(ref_b - top))
            total = jnp.sum(
                mine_ref[HD : HD + 8, at] * gain_a + other_ref[HD : HD + 8, at] * gain_b,
                axis=0,
                keepdims=True,
            )
            attended = (mine_ref[0:HD, at] * gain_a + other_ref[0:HD, at] * gain_b) / total
            halves.append(attended.astype(jnp.bfloat16))
        banded = dot_nt(choose_ref[...], jnp.concatenate(halves, axis=0))
        upper, lower = (banded[:, n * HD : (n + 1) * HD].reshape(BANDS, WIDE, 8, HD) for n in range(2))
        rows = jnp.concatenate([upper, lower], axis=2).astype(jnp.bfloat16)
        out_ref[frame * BANDS : (frame + 1) * BANDS] = rows.reshape(BANDS, WIDE * 16, HD)


def combine(mine, other):
    choose = jnp.asarray(band_selection(), jnp.bfloat16)
    return pl.pallas_call(
        combine_kernel,
        out_shape=jax.ShapeDtypeStruct((2 * BANDS, WIDE * 16, HD), jnp.bfloat16),
        compiler_params=pltpu.CompilerParams(vmem_limit_bytes=20 * MIB),
    )(mine, other, choose)


def window_selection():
    chosen = np.zeros((3, 4 * C_LAT, 2, 4, C_LAT), np.float32)
    for i in range(2):
        for col in range(4):
            side, j = divmod(col + 1, 2)
            for ch in range(C_LAT):
                chosen[side, 4 * ch + 2 * i + j, i, col, ch] = 1.0
    return chosen.reshape(3, 4 * C_LAT, 128)


def row_order():
    chosen = np.zeros((BAND, PH, BAND, PH), np.float32)
    for col in range(BAND):
        for row in range(PH):
            pair, core, low = (row // 4, row // 2 % 2, row % 2)
            chosen[col, row, col, core * 16 + pair * 2 + low] = 1.0
    return chosen.reshape(BAND * PH, BAND * PH)


TILE_N = 512


def project_kernel(
    band_ref, x_ref, w_ref, shift_ref, scale_ref, final_ref, choose_ref, order_ref, out_ref, rows_ref, proj_ref, tiles_ref, sems
):
    tiles = D // TILE_N

    def fetch(n):
        return pltpu.make_async_copy(w_ref.at[:, pl.ds(n * TILE_N, TILE_N)], tiles_ref.at[n], sems.at[n])

    for n in range(tiles):
        fetch(n).start()
    for head in range(HEADS):
        for core in range(2):
            for col in range(WIDE):
                at = col * PH + core * 16
                rows_ref[at : at + 16, head * HD : (head + 1) * HD] = x_ref[head, core, col * 16 : (col + 1) * 16, :]
    total = 0.0
    square = 0.0
    for n in range(tiles):
        fetch(n).wait()
        part = jnp.dot(rows_ref[...], tiles_ref[n], preferred_element_type=jnp.float32)
        proj_ref[n] = part
        part_sum = jnp.sum(part, axis=1, keepdims=True)
        if n == 0:
            near = part_sum / TILE_N
        total = total + part_sum
        square = square + jnp.sum((part - near) * (part - near), axis=1, keepdims=True)
    mean = total / D
    variance = square / D - (mean - near) * (mean - near)
    inverse = 1.0 / jnp.sqrt(variance + 1e-06)

    def reduce(n, patches):
        at = pl.ds(pl.multiple_of(n * TILE_N, TILE_N), TILE_N)
        normed = (proj_ref[n] - mean) * inverse * (1.0 + scale_ref[:, at]) + shift_ref[:, at]
        return patches + jnp.dot(normed.astype(jnp.bfloat16), final_ref[at, :], preferred_element_type=jnp.float32)

    patches = lax.fori_loop(0, tiles, reduce, jnp.zeros((PH * WIDE, 4 * C_LAT), jnp.float32), unroll=2)
    place = lax.broadcasted_iota(jnp.int32, patches.shape, 0) // PH + (band_ref[0] * BAND - 1)
    patches = jnp.where((place >= 0) & (place < PW), patches, 0.0).astype(jnp.bfloat16)
    wide = 0.0
    for side in range(3):
        moved = patches[side * PH : (side + BAND) * PH]
        wide = wide + jnp.dot(moved, choose_ref[side], preferred_element_type=jnp.float32)
    wide = jnp.dot(order_ref[...], wide.astype(jnp.bfloat16), preferred_element_type=jnp.float32)
    out_ref[...] = wide.astype(jnp.bfloat16)


def project(band, gathered, w_out, shift_vec, scale_vec, w_final):
    choose = jnp.asarray(window_selection(), jnp.bfloat16)
    order = jnp.asarray(row_order(), jnp.bfloat16)
    vmem = pl.BlockSpec(memory_space=pltpu.VMEM)
    return pl.pallas_call(
        project_kernel,
        in_specs=[pl.BlockSpec(memory_space=pltpu.SMEM), vmem, pl.BlockSpec(memory_space=pl.ANY)] + [vmem] * 5,
        out_specs=vmem,
        out_shape=jax.ShapeDtypeStruct((BAND * PH, 128), jnp.bfloat16),
        scratch_shapes=[
            pltpu.VMEM((PH * WIDE, HEADS * HD), jnp.bfloat16),
            pltpu.VMEM((D // TILE_N, PH * WIDE, TILE_N), jnp.float32),
            pltpu.VMEM((D // TILE_N, HEADS * HD, TILE_N), jnp.bfloat16),
            pltpu.SemaphoreType.DMA((D // TILE_N,)),
        ],
        compiler_params=pltpu.CompilerParams(vmem_limit_bytes=52 * MIB),
    )(band, gathered, w_out, shift_vec.reshape(1, D), scale_vec.reshape(1, D), w_final, choose, order)


def conv_kernel(frame_ref, now_ref, one_ref, two_ref, w_ref, out_ref, taps_ref, spread_ref):
    rows = BAND * PH
    taps_ref[...] = jnp.zeros_like(taps_ref)
    for odd in range(2):
        for a in range(3):
            for b in range(3):
                y = odd + b - 1
                offset = {-1: 192, 0: 0, 1: 64, 2: 128}[y]
                for j in range(2):
                    for e in range(3):
                        at = offset + (j + e) * C_LAT
                        tap = ((a * 3 + b) * 3 + e) * C_LAT
                        taps_ref[odd, a, at : at + C_LAT, j * C_VAE : (j + 1) * C_VAE] = w_ref[tap : tap + C_LAT, :]
    frame = frame_ref[0]
    now = now_ref[...].astype(jnp.float32)
    one = jnp.where(frame >= 1, one_ref[...].astype(jnp.float32), now)
    two = jnp.where(frame >= 2, two_ref[...].astype(jnp.float32), one)
    row = lax.rem(lax.broadcasted_iota(jnp.int32, (rows, 128), 0), PH)
    for odd in range(2):
        result = jnp.zeros((rows, 2 * C_VAE), jnp.float32)
        for a, grid in enumerate((two, one, now)):
            if odd == 0:
                beside = jnp.where(row == 0, 0.0, pltpu.roll(grid, 1, 0))
            else:
                beside = jnp.where(row == PH - 1, 0.0, pltpu.roll(grid, rows - 1, 0))
            window = jnp.concatenate([grid, beside], axis=1).astype(jnp.bfloat16)
            result = result + jnp.dot(window, taps_ref[odd, a], preferred_element_type=jnp.float32)
        for col in range(BAND):
            for j in range(2):
                for part in range(C_VAE // 128):
                    at = j * C_VAE + part * 128
                    spread_ref[part, pl.ds((2 * col + j) * 2 * PH + odd, PH, stride=2), :] = result[
                        col * PH : (col + 1) * PH, at : at + 128
                    ]
    for part in range(C_VAE // 128):
        final = spread_ref[part].reshape(2 * BAND, 2 * PH, 128)
        out_ref[:, :, part * 128 : (part + 1) * 128] = final.astype(jnp.bfloat16)


def convolve(frame, now, one, two, w_conv):
    return pl.pallas_call(
        conv_kernel,
        grid=(1,),
        in_specs=[pl.BlockSpec(memory_space=pltpu.SMEM)]
        + [pl.BlockSpec((BAND * PH, 128), lambda i: (0, 0))] * 3
        + [pl.BlockSpec((27 * C_LAT, C_VAE), lambda i: (0, 0))],
        out_specs=pl.BlockSpec((2 * BAND, 2 * PH, C_VAE), lambda i: (0, 0, 0)),
        out_shape=jax.ShapeDtypeStruct((2 * BAND, 2 * PH, C_VAE), jnp.bfloat16),
        scratch_shapes=[
            pltpu.VMEM((2, 3, 256, 2 * C_VAE), jnp.bfloat16),
            pltpu.VMEM((C_VAE // 128, 4 * BAND * PH, 128), jnp.float32),
        ],
        compiler_params=pltpu.CompilerParams(vmem_limit_bytes=24 * MIB),
    )(frame, now, one, two, w_conv.reshape(27 * C_LAT, C_VAE))


def ring(x, axis, by):
    count = lax.axis_size(axis)
    return lax.ppermute(x, axis, [(i, (i + by) % count) for i in range(count)])


def later(x, by):
    count = lax.axis_size(("y", "zl"))
    return lax.ppermute(x, ("y", "zl"), [(i, i + by) for i in range(count - by)])


def per_device(queries, key_rows, value_rows, w_out, shift_vec, scale_vec, w_final, w_conv):
    tokens = queries.shape[0]

    def by_head(x):
        return x.reshape(tokens, HEADS, HD).transpose(1, 0, 2)

    outgoing = jnp.concatenate([by_head(key_rows), by_head(value_rows), by_head(queries)], axis=2)
    incoming = lax.all_to_all(outgoing, PLANE, 0, 0, tiled=True).reshape(HEADS * tokens, 3 * HD)
    half = HEADS * tokens // 2
    kv = incoming[:, : 2 * HD]
    kv_a, kv_b = (kv[:half], kv[half:])
    q_mine = incoming[:, 2 * HD :]
    below_a, above_b = (ring(kv_a, "y", 1), ring(kv_b, "y", -1))
    q_theirs = ring(q_mine, "c", 1)
    columns = 4 * half
    state = attend(q_mine, [kv_a, kv_b], columns=columns)
    kv_a, kv_b, q_theirs, state = lax.optimization_barrier((kv_a, kv_b, q_theirs, state))
    below_b, above_a = (ring(kv_b, "y", 1), ring(kv_a, "y", -1))
    state = attend(q_theirs, [kv_a, kv_b], columns=columns, offset=2 * half, fill=state)
    q_all = jnp.concatenate([q_mine, q_theirs], axis=0)
    below_a, above_b, state = lax.optimization_barrier((below_a, above_b, state))
    far_a, far_b = (ring(below_a, "y", 1), ring(above_b, "y", -1))
    state = attend(q_all, [below_a, above_b], state)
    below_b, above_a, state = lax.optimization_barrier((below_b, above_a, state))
    state = attend(q_all, [below_b, above_a], state)
    far_a, far_b, state = lax.optimization_barrier((far_a, far_b, state))
    theirs = attend(q_theirs, [far_a, far_b], state, offset=2 * half)
    theirs = ring(theirs, "c", 1)
    mine = attend(q_mine, [far_a, far_b], state)
    banded = combine(mine, theirs)
    gathered = lax.all_to_all(banded, ("zl", "x", "zh", "c"), 0, 0, tiled=True)
    gathered = gathered.reshape(HEADS, 2, WIDE * 16, HD)
    band = lax.axis_index(("x", "zh", "c")).astype(jnp.int32).reshape(1)
    frame = lax.axis_index(("y", "zl")).astype(jnp.int32).reshape(1)
    now = project(band, gathered, w_out, shift_vec, scale_vec, w_final)
    decoded = convolve(frame, now, later(now, 1), later(now, 2), w_conv)
    return decoded.transpose(1, 0, 2)[None]


def solution(mesh):
    fine = Mesh(mesh.devices.reshape(SIZES), AXES)
    rows = P(AXES, None)
    return jax.shard_map(
        per_device,
        mesh=fine,
        in_specs=(rows, rows, rows, P(), P(), P(), P(), P()),
        out_specs=P(("y", "zl"), None, ("x", "zh", "c"), None),
        check_vma=False,
    )
```

```python
import functools

import jax
import jax.numpy as jnp
import numpy as np
from jax import lax
from jax.experimental import pallas as pl
from jax.experimental.pallas import tpu as pltpu
from jax.sharding import Mesh, PartitionSpec as P

HD = 128
HEADS = 16
D = 3072
C_LAT = 16
C_VAE = 512
PW = 80
PH = 32
BANDS = 16
BAND = 5
WIDE = 7
ROWS = 8 * PW
AXES = ("y", "zl", "x", "zh", "c")
SIZES = (4, 2, 4, 2, 2)
PLANE = ("zl", "x", "zh")
SCALE_LOG2 = HD ** -0.5 * 1.4426950408889634
LIMIT = 1e30
NT = (((1,), (1,)), ((), ()))
STATE = HD + 16
MIB = 2 ** 20
ATTEND_MIB = 36


def dot_nt(a, b):
    return lax.dot_general(a, b, NT, preferred_element_type=jnp.float32)


def attention_kernel(*refs, pieces, first, filled, block, read, write):
    here = pl.multiple_of(pl.program_id(0) * block, block)
    q_ref = refs[0].at[pl.ds(here, block)]
    kv_refs = refs[1 : 1 + pieces]
    rest = refs[1 + pieces :]
    if filled:
        rest = rest[1:]
    if first:
        out_ref, keys_ref, vt_ref = rest
    else:
        in_ref, out_ref, keys_ref, vt_ref = rest
        in_ref = in_ref.at[:, pl.ds(pl.multiple_of(read + here, block), block)]
    out_ref = out_ref.at[:, pl.ds(pl.multiple_of(write + here, block), block)]
    starts = [0]
    for kv in kv_refs:
        starts.append(starts[-1] + kv.shape[0])

    q_scaled = q_ref[...].astype(jnp.float32) * SCALE_LOG2
    q_hi = q_scaled.astype(jnp.bfloat16)
    q_lo = (q_scaled - q_hi.astype(jnp.float32)).astype(jnp.bfloat16)
    q_pair = jnp.concatenate([q_hi, q_lo], axis=1)
    cols = q_pair.shape[0]

    def scores_of(keys):
        return dot_nt(jnp.concatenate([keys, keys], axis=1), q_pair)

    if first:
        reference = jnp.max(scores_of(kv_refs[0][0:256, :HD]), axis=0, keepdims=True)
        total = jnp.zeros((8, cols), jnp.float32)
        acc = jnp.zeros((HD, cols), jnp.float32)
    else:
        reference = in_ref[HD + 8 : HD + 9, :]
        total = in_ref[HD : HD + 8, :]
        acc = in_ref[0:HD, :]
    for n, kv in enumerate(kv_refs):
        size = kv.shape[0]
        step = min(size, 1280)
        for at in range(0, size, step):
            weights = jnp.exp2(scores_of(kv[at : at + step, :HD]) - reference)
            total = total + jnp.sum(weights.reshape(step // 8, 8, cols), axis=0)
            acc = acc + jnp.dot(
                kv[at : at + step, HD:].T,
                weights.astype(jnp.bfloat16),
                preferred_element_type=jnp.float32,
            )
    out_ref[0:HD, :] = acc
    out_ref[HD : HD + 8, :] = total
    out_ref[HD + 8 :, :] = jnp.broadcast_to(reference, (8, cols))
    safe = jnp.max(total) < LIMIT

    @pl.when(jnp.logical_not(safe))
    def _():
        if first:
            out_ref[0 : HD + 8, :] = jnp.zeros((HD + 8, cols), jnp.float32)
        else:
            out_ref[...] = in_ref[...]
        for n, kv in enumerate(kv_refs):
            keys_ref[starts[n] : starts[n + 1], :] = kv[:, :HD]
            vt_ref[:, starts[n] : starts[n + 1]] = kv[:, HD:].T

        def absorb(i, carry):
            at = pl.multiple_of(i * 128, 128)
            scores = scores_of(keys_ref[pl.ds(at, 128), :])
            old = out_ref[HD + 8 : HD + 9, :]
            new = jnp.maximum(old, jnp.max(scores, axis=0, keepdims=True))
            rescale = jnp.exp2(old - new)
            weights = jnp.exp2(scores - new)
            out_ref[HD : HD + 8, :] = out_ref[HD : HD + 8, :] * rescale + jnp.sum(
                weights.reshape(16, 8, cols), axis=0
            )
            out_ref[0:HD, :] = out_ref[0:HD, :] * rescale + jnp.dot(
                vt_ref[:, pl.ds(at, 128)], weights.astype(jnp.bfloat16), preferred_element_type=jnp.float32
            )
            out_ref[HD + 8 :, :] = jnp.broadcast_to(new, (8, cols))
            return carry

        lax.fori_loop(0, starts[-1] // 128, absorb, 0)


def attend(q, kvs, state=None, columns=None, offset=0, fill=None, block=1280):
    rows = q.shape[0]
    first = state is None
    keys = sum(kv.shape[0] for kv in kvs)
    shift = offset // block
    write = shift if columns else 0
    vmem = pl.BlockSpec(memory_space=pltpu.VMEM)
    args = [q] + list(kvs)
    aliases = {}
    if not first:
        args.append(state)
    if fill is not None:
        aliases = {len(args): 0}
        args.append(fill)
    return pl.pallas_call(
        functools.partial(
            attention_kernel,
            pieces=len(kvs),
            first=first,
            filled=fill is not None,
            block=block,
            read=shift * block,
            write=write * block,
        ),
        grid=(rows // block,),
        in_specs=[vmem] * len(args),
        out_specs=vmem,
        out_shape=jax.ShapeDtypeStruct((STATE, columns or rows), jnp.float32),
        scratch_shapes=[pltpu.VMEM((keys, HD), jnp.bfloat16), pltpu.VMEM((HD, keys), jnp.bfloat16)],
        input_output_aliases=aliases,
        compiler_params=pltpu.CompilerParams(vmem_limit_bytes=ATTEND_MIB * MIB),
        cost_estimate=pl.CostEstimate(
            flops=rows * keys * 6 * HD,
            bytes_accessed=rows * 1408 + keys * 512,
            transcendentals=rows * keys,
        ),
    )(*args)


def band_selection():
    chosen = np.zeros((BANDS, WIDE, 8, ROWS), np.float32)
    for band in range(BANDS):
        for col in range(WIDE):
            place = band * BAND - 1 + col
            if 0 <= place < PW:
                for row in range(8):
                    chosen[band, col, row, row * PW + place] = 1.0
    return chosen.reshape(BANDS * WIDE * 8, ROWS)


def combine_kernel(mine_ref, other_ref, choose_ref, out_ref):
    for frame in range(2):
        halves = []
        for half in range(2):
            at = slice((2 * frame + half) * ROWS, (2 * frame + half + 1) * ROWS)
            ref_a, ref_b = (mine_ref[HD + 8 : HD + 9, at], other_ref[HD + 8 : HD + 9, at])
            top = jnp.maximum(ref_a, ref_b)
            gain_a, gain_b = (jnp.exp2(ref_a - top), jnp.exp2(ref_b - top))
            total = jnp.sum(
                mine_ref[HD : HD + 8, at] * gain_a + other_ref[HD : HD + 8, at] * gain_b,
                axis=0,
                keepdims=True,
            )
            attended = (mine_ref[0:HD, at] * gain_a + other_ref[0:HD, at] * gain_b) / total
            halves.append(attended.astype(jnp.bfloat16))
        banded = dot_nt(choose_ref[...], jnp.concatenate(halves, axis=0))
        upper, lower = (banded[:, n * HD : (n + 1) * HD].reshape(BANDS, WIDE, 8, HD) for n in range(2))
        rows = jnp.concatenate([upper, lower], axis=2).astype(jnp.bfloat16)
        out_ref[frame * BANDS : (frame + 1) * BANDS] = rows.reshape(BANDS, WIDE * 16, HD)


def combine(mine, other):
    choose = jnp.asarray(band_selection(), jnp.bfloat16)
    return pl.pallas_call(
        combine_kernel,
        out_shape=jax.ShapeDtypeStruct((2 * BANDS, WIDE * 16, HD), jnp.bfloat16),
        compiler_params=pltpu.CompilerParams(vmem_limit_bytes=20 * MIB),
    )(mine, other, choose)


def window_selection():
    chosen = np.zeros((3, 4 * C_LAT, 2, 4, C_LAT), np.float32)
    for i in range(2):
        for col in range(4):
            side, j = divmod(col + 1, 2)
            for ch in range(C_LAT):
                chosen[side, 4 * ch + 2 * i + j, i, col, ch] = 1.0
    return chosen.reshape(3, 4 * C_LAT, 128)


def row_order():
    chosen = np.zeros((BAND, PH, BAND, PH), np.float32)
    for col in range(BAND):
        for row in range(PH):
            pair, core, low = (row // 4, row // 2 % 2, row % 2)
            chosen[col, row, col, core * 16 + pair * 2 + low] = 1.0
    return chosen.reshape(BAND * PH, BAND * PH)


TILE_N = 512
AHEAD = 4


def project_kernel(
    band_ref, x_ref, w_ref, shift_ref, scale_ref, final_ref, choose_ref, order_ref, out_ref, rows_ref, proj_ref, tiles_ref, sems
):
    tiles = D // TILE_N

    def fetch(n):
        return pltpu.make_async_copy(w_ref.at[:, pl.ds(n * TILE_N, TILE_N)], tiles_ref.at[n], sems.at[n])

    for n in range(AHEAD):
        fetch(n).start()
    for head in range(HEADS):
        for core in range(2):
            for col in range(WIDE):
                at = col * PH + core * 16
                rows_ref[at : at + 16, head * HD : (head + 1) * HD] = x_ref[head, core, col * 16 : (col + 1) * 16, :]
    total = 0.0
    square = 0.0
    for n in range(tiles):
        fetch(n).wait()
        if n + AHEAD < tiles:
            fetch(n + AHEAD).start()
        part = jnp.dot(rows_ref[...], tiles_ref[n], preferred_element_type=jnp.float32)
        proj_ref[n] = part
        part_sum = jnp.sum(part, axis=1, keepdims=True)
        if n == 0:
            near = part_sum / TILE_N
        total = total + part_sum
        square = square + jnp.sum((part - near) * (part - near), axis=1, keepdims=True)
    mean = total / D
    variance = square / D - (mean - near) * (mean - near)
    inverse = 1.0 / jnp.sqrt(variance + 1e-06)

    def reduce(n, patches):
        at = slice(n * TILE_N, (n + 1) * TILE_N)
        normed = (proj_ref[n] - mean) * inverse * (1.0 + scale_ref[:, at]) + shift_ref[:, at]
        return patches + jnp.dot(normed.astype(jnp.bfloat16), final_ref[at, :], preferred_element_type=jnp.float32)

    patches = jnp.zeros((PH * WIDE, 4 * C_LAT), jnp.float32)
    for n in range(tiles):
        patches = reduce(n, patches)
    place = lax.broadcasted_iota(jnp.int32, patches.shape, 0) // PH + (band_ref[0] * BAND - 1)
    patches = jnp.where((place >= 0) & (place < PW), patches, 0.0).astype(jnp.bfloat16)
    wide = 0.0
    for side in range(3):
        moved = patches[side * PH : (side + BAND) * PH]
        wide = wide + jnp.dot(moved, choose_ref[side], preferred_element_type=jnp.float32)
    wide = jnp.dot(order_ref[...], wide.astype(jnp.bfloat16), preferred_element_type=jnp.float32)
    out_ref[...] = wide.astype(jnp.bfloat16)


def project(band, gathered, w_out, shift_vec, scale_vec, w_final):
    choose = jnp.asarray(window_selection(), jnp.bfloat16)
    order = jnp.asarray(row_order(), jnp.bfloat16)
    vmem = pl.BlockSpec(memory_space=pltpu.VMEM)
    return pl.pallas_call(
        project_kernel,
        in_specs=[pl.BlockSpec(memory_space=pltpu.SMEM), vmem, pl.BlockSpec(memory_space=pl.ANY)] + [vmem] * 5,
        out_specs=vmem,
        out_shape=jax.ShapeDtypeStruct((BAND * PH, 128), jnp.bfloat16),
        scratch_shapes=[
            pltpu.VMEM((PH * WIDE, HEADS * HD), jnp.bfloat16),
            pltpu.VMEM((D // TILE_N, PH * WIDE, TILE_N), jnp.float32),
            pltpu.VMEM((D // TILE_N, HEADS * HD, TILE_N), jnp.bfloat16),
            pltpu.SemaphoreType.DMA((D // TILE_N,)),
        ],
        compiler_params=pltpu.CompilerParams(vmem_limit_bytes=52 * MIB),
    )(band, gathered, w_out, shift_vec.reshape(1, D), scale_vec.reshape(1, D), w_final, choose, order)


def windows_of(grid, odd):
    rows = BAND * PH
    row = lax.rem(lax.broadcasted_iota(jnp.int32, (rows, 128), 0), PH)
    if odd == 0:
        beside = jnp.where(row == 0, 0.0, pltpu.roll(grid, 1, 0))
    else:
        beside = jnp.where(row == PH - 1, 0.0, pltpu.roll(grid, rows - 1, 0))
    return jnp.concatenate([grid, beside], axis=1).astype(jnp.bfloat16)


def conv_now_kernel(now_ref, w_ref, part_ref, taps_ref, last_ref):
    for taps, frames in ((taps_ref, (0, 1)), (last_ref, (2,))):
        taps[...] = jnp.zeros_like(taps)
        for odd in range(2):
            for n, a in enumerate(frames):
                for b in range(3):
                    y = odd + b - 1
                    offset = {-1: 192, 0: 0, 1: 64, 2: 128}[y]
                    for j in range(2):
                        for e in range(3):
                            at = offset + (j + e) * C_LAT
                            tap = ((a * 3 + b) * 3 + e) * C_LAT
                            taps[odd, n, at : at + C_LAT, j * C_VAE : (j + 1) * C_VAE] = w_ref[tap : tap + C_LAT, :]
    now = now_ref[...].astype(jnp.float32)
    for odd in range(2):
        part_ref[odd] = jnp.dot(windows_of(now, odd), last_ref[odd, 0], preferred_element_type=jnp.float32)


def conv_kernel(frame_ref, now_ref, one_ref, two_ref, part_ref, taps_ref, out_ref, spread_ref):
    frame = frame_ref[0]
    now = now_ref[...].astype(jnp.float32)
    one = jnp.where(frame >= 1, one_ref[...].astype(jnp.float32), now)
    two = jnp.where(frame >= 2, two_ref[...].astype(jnp.float32), one)
    for odd in range(2):
        result = part_ref[odd]
        for a, grid in enumerate((two, one)):
            result = result + jnp.dot(windows_of(grid, odd), taps_ref[odd, a], preferred_element_type=jnp.float32)
        for col in range(BAND):
            for j in range(2):
                for part in range(C_VAE // 128):
                    at = j * C_VAE + part * 128
                    spread_ref[part, pl.ds((2 * col + j) * 2 * PH + odd, PH, stride=2), :] = result[
                        col * PH : (col + 1) * PH, at : at + 128
                    ]
    for part in range(C_VAE // 128):
        final = spread_ref[part].reshape(2 * BAND, 2 * PH, 128)
        out_ref[:, :, part * 128 : (part + 1) * 128] = final.astype(jnp.bfloat16)


def convolve(frame, now, one, two, w_conv):
    rows = BAND * PH
    vmem = pl.BlockSpec(memory_space=pltpu.VMEM)
    taps = w_conv.reshape(27 * C_LAT, C_VAE)
    part, taps = pl.pallas_call(
        conv_now_kernel,
        in_specs=[vmem] * 2,
        out_specs=[vmem] * 2,
        out_shape=[
            jax.ShapeDtypeStruct((2, rows, 2 * C_VAE), jnp.float32),
            jax.ShapeDtypeStruct((2, 2, 256, 2 * C_VAE), jnp.bfloat16),
        ],
        scratch_shapes=[pltpu.VMEM((2, 1, 256, 2 * C_VAE), jnp.bfloat16)],
        compiler_params=pltpu.CompilerParams(vmem_limit_bytes=24 * MIB),
        cost_estimate=pl.CostEstimate(flops=rows * 2 ** 20, bytes_accessed=2 ** 22, transcendentals=0),
    )(now, taps)
    return pl.pallas_call(
        conv_kernel,
        grid=(1,),
        in_specs=[pl.BlockSpec(memory_space=pltpu.SMEM)] + [vmem] * 5,
        out_specs=pl.BlockSpec((2 * BAND, 2 * PH, C_VAE), lambda i: (0, 0, 0)),
        out_shape=jax.ShapeDtypeStruct((2 * BAND, 2 * PH, C_VAE), jnp.bfloat16),
        scratch_shapes=[pltpu.VMEM((C_VAE // 128, 4 * BAND * PH, 128), jnp.float32)],
        compiler_params=pltpu.CompilerParams(vmem_limit_bytes=24 * MIB),
    )(frame, now, one, two, part, taps)


def ring(x, axis, by):
    count = lax.axis_size(axis)
    return lax.ppermute(x, axis, [(i, (i + by) % count) for i in range(count)])


def later(x, by):
    count = lax.axis_size(("y", "zl"))
    return lax.ppermute(x, ("y", "zl"), [(i, i + by) for i in range(count - by)])


def per_device(queries, key_rows, value_rows, w_out, shift_vec, scale_vec, w_final, w_conv):
    tokens = queries.shape[0]

    def by_head(x):
        return x.reshape(tokens, HEADS, HD).transpose(1, 0, 2)

    outgoing = jnp.concatenate([by_head(key_rows), by_head(value_rows), by_head(queries)], axis=2)
    incoming = lax.all_to_all(outgoing, PLANE, 0, 0, tiled=True).reshape(HEADS * tokens, 3 * HD)
    half = HEADS * tokens // 2
    kv = incoming[:, : 2 * HD]
    kv_a, kv_b = (kv[:half], kv[half:])
    q_mine = incoming[:, 2 * HD :]
    below_a, above_b = (ring(kv_a, "y", 1), ring(kv_b, "y", -1))
    q_theirs = ring(q_mine, "c", 1)
    columns = 4 * half
    state = attend(q_mine, [kv_a, kv_b], columns=columns)
    kv_a, kv_b, q_theirs, state = lax.optimization_barrier((kv_a, kv_b, q_theirs, state))
    below_b, above_a = (ring(kv_b, "y", 1), ring(kv_a, "y", -1))
    state = attend(q_theirs, [kv_a, kv_b], columns=columns, offset=2 * half, fill=state)
    q_all = jnp.concatenate([q_mine, q_theirs], axis=0)
    below_a, above_b, state = lax.optimization_barrier((below_a, above_b, state))
    far_a, far_b = (ring(below_a, "y", 1), ring(above_b, "y", -1))
    state = attend(q_all, [below_a, above_b], state)
    below_b, above_a, state = lax.optimization_barrier((below_b, above_a, state))
    state = attend(q_all, [below_b, above_a], state)
    far_a, far_b, state = lax.optimization_barrier((far_a, far_b, state))
    theirs = attend(q_theirs, [far_a, far_b], state, offset=2 * half)
    theirs = ring(theirs, "c", 1)
    mine = attend(q_mine, [far_a, far_b], state)
    banded = combine(mine, theirs)
    gathered = lax.all_to_all(banded, ("zl", "x", "zh", "c"), 0, 0, tiled=True)
    gathered = gathered.reshape(HEADS, 2, WIDE * 16, HD)
    band = lax.axis_index(("x", "zh", "c")).astype(jnp.int32).reshape(1)
    frame = lax.axis_index(("y", "zl")).astype(jnp.int32).reshape(1)
    now = project(band, gathered, w_out, shift_vec, scale_vec, w_final)
    decoded = convolve(frame, now, later(now, 1), later(now, 2), w_conv)
    return decoded.transpose(1, 0, 2)[None]


def solution(mesh):
    fine = Mesh(mesh.devices.reshape(SIZES), AXES)
    rows = P(AXES, None)
    return jax.shard_map(
        per_device,
        mesh=fine,
        in_specs=(rows, rows, rows, P(), P(), P(), P(), P()),
        out_specs=P(("y", "zl"), None, ("x", "zh", "c"), None),
        check_vma=False,
    )
```

```python
import functools

import jax
import jax.numpy as jnp
import numpy as np
from jax import lax
from jax.experimental import pallas as pl
from jax.experimental.pallas import tpu as pltpu
from jax.sharding import Mesh, PartitionSpec as P

HD = 128
HEADS = 16
D = 3072
C_LAT = 16
C_VAE = 512
PW = 80
PH = 32
BANDS = 16
BAND = 5
WIDE = 7
ROWS = 8 * PW
AXES = ("y", "zl", "x", "zh", "c")
SIZES = (4, 2, 4, 2, 2)
PLANE = ("zl", "x", "zh")
SCALE_LOG2 = HD ** -0.5 * 1.4426950408889634
LIMIT = 1e30
NT = (((1,), (1,)), ((), ()))
STATE = HD + 16
MIB = 2 ** 20
ATTEND_MIB = 36


def dot_nt(a, b):
    return lax.dot_general(a, b, NT, preferred_element_type=jnp.float32)


def attention_kernel(*refs, pieces, first, filled, block, read, write):
    here = pl.multiple_of(pl.program_id(0) * block, block)
    q_ref = refs[0].at[pl.ds(here, block)]
    kv_refs = refs[1 : 1 + pieces]
    rest = refs[1 + pieces :]
    if filled:
        rest = rest[1:]
    if first:
        out_ref, keys_ref, vt_ref = rest
    else:
        in_ref, out_ref, keys_ref, vt_ref = rest
        in_ref = in_ref.at[:, pl.ds(pl.multiple_of(read + here, block), block)]
    out_ref = out_ref.at[:, pl.ds(pl.multiple_of(write + here, block), block)]
    starts = [0]
    for kv in kv_refs:
        starts.append(starts[-1] + kv.shape[0])

    q_scaled = q_ref[...].astype(jnp.float32) * SCALE_LOG2
    q_hi = q_scaled.astype(jnp.bfloat16)
    q_lo = (q_scaled - q_hi.astype(jnp.float32)).astype(jnp.bfloat16)
    q_pair = jnp.concatenate([q_hi, q_lo], axis=1)
    cols = q_pair.shape[0]

    def scores_of(keys):
        return dot_nt(jnp.concatenate([keys, keys], axis=1), q_pair)

    if first:
        reference = jnp.max(scores_of(kv_refs[0][0:256, :HD]), axis=0, keepdims=True)
        total = jnp.zeros((8, cols), jnp.float32)
        acc = jnp.zeros((HD, cols), jnp.float32)
    else:
        reference = in_ref[HD + 8 : HD + 9, :]
        total = in_ref[HD : HD + 8, :]
        acc = in_ref[0:HD, :]
    for n, kv in enumerate(kv_refs):
        size = kv.shape[0]
        step = min(size, 1280)
        for at in range(0, size, step):
            weights = jnp.exp2(scores_of(kv[at : at + step, :HD]) - reference)
            total = total + jnp.sum(weights.reshape(step // 8, 8, cols), axis=0)
            acc = acc + jnp.dot(
                kv[at : at + step, HD:].T,
                weights.astype(jnp.bfloat16),
                preferred_element_type=jnp.float32,
            )
    out_ref[0:HD, :] = acc
    out_ref[HD : HD + 8, :] = total
    out_ref[HD + 8 :, :] = jnp.broadcast_to(reference, (8, cols))
    safe = jnp.max(total) < LIMIT

    @pl.when(jnp.logical_not(safe))
    def _():
        if first:
            out_ref[0 : HD + 8, :] = jnp.zeros((HD + 8, cols), jnp.float32)
        else:
            out_ref[...] = in_ref[...]
        for n, kv in enumerate(kv_refs):
            keys_ref[starts[n] : starts[n + 1], :] = kv[:, :HD]
            vt_ref[:, starts[n] : starts[n + 1]] = kv[:, HD:].T

        def absorb(i, carry):
            at = pl.multiple_of(i * 128, 128)
            scores = scores_of(keys_ref[pl.ds(at, 128), :])
            old = out_ref[HD + 8 : HD + 9, :]
            new = jnp.maximum(old, jnp.max(scores, axis=0, keepdims=True))
            rescale = jnp.exp2(old - new)
            weights = jnp.exp2(scores - new)
            out_ref[HD : HD + 8, :] = out_ref[HD : HD + 8, :] * rescale + jnp.sum(
                weights.reshape(16, 8, cols), axis=0
            )
            out_ref[0:HD, :] = out_ref[0:HD, :] * rescale + jnp.dot(
                vt_ref[:, pl.ds(at, 128)], weights.astype(jnp.bfloat16), preferred_element_type=jnp.float32
            )
            out_ref[HD + 8 :, :] = jnp.broadcast_to(new, (8, cols))
            return carry

        lax.fori_loop(0, starts[-1] // 128, absorb, 0)


def attend(q, kvs, state=None, columns=None, offset=0, fill=None, block=1280):
    rows = q.shape[0]
    first = state is None
    keys = sum(kv.shape[0] for kv in kvs)
    shift = offset // block
    write = shift if columns else 0
    vmem = pl.BlockSpec(memory_space=pltpu.VMEM)
    args = [q] + list(kvs)
    aliases = {}
    if not first:
        args.append(state)
    if fill is not None:
        aliases = {len(args): 0}
        args.append(fill)
    return pl.pallas_call(
        functools.partial(
            attention_kernel,
            pieces=len(kvs),
            first=first,
            filled=fill is not None,
            block=block,
            read=shift * block,
            write=write * block,
        ),
        grid=(rows // block,),
        in_specs=[vmem] * len(args),
        out_specs=vmem,
        out_shape=jax.ShapeDtypeStruct((STATE, columns or rows), jnp.float32),
        scratch_shapes=[pltpu.VMEM((keys, HD), jnp.bfloat16), pltpu.VMEM((HD, keys), jnp.bfloat16)],
        input_output_aliases=aliases,
        compiler_params=pltpu.CompilerParams(vmem_limit_bytes=ATTEND_MIB * MIB),
        cost_estimate=pl.CostEstimate(
            flops=rows * keys * 6 * HD,
            bytes_accessed=rows * 1408 + keys * 512,
            transcendentals=rows * keys,
        ),
    )(*args)


def band_selection():
    chosen = np.zeros((BANDS, WIDE, 8, ROWS), np.float32)
    for band in range(BANDS):
        for col in range(WIDE):
            place = band * BAND - 1 + col
            if 0 <= place < PW:
                for row in range(8):
                    chosen[band, col, row, row * PW + place] = 1.0
    return chosen.reshape(BANDS * WIDE * 8, ROWS)


def combine_kernel(mine_ref, other_ref, choose_ref, out_ref):
    frame = pl.program_id(0)
    halves = []
    for half in range(2):
        at = pl.ds(pl.multiple_of((2 * frame + half) * ROWS, ROWS), ROWS)
        ref_a, ref_b = (mine_ref[HD + 8 : HD + 9, at], other_ref[HD + 8 : HD + 9, at])
        top = jnp.maximum(ref_a, ref_b)
        gain_a, gain_b = (jnp.exp2(ref_a - top), jnp.exp2(ref_b - top))
        total = jnp.sum(
            mine_ref[HD : HD + 8, at] * gain_a + other_ref[HD : HD + 8, at] * gain_b,
            axis=0,
            keepdims=True,
        )
        attended = (mine_ref[0:HD, at] * gain_a + other_ref[0:HD, at] * gain_b) / total
        halves.append(attended.astype(jnp.bfloat16))
    banded = dot_nt(choose_ref[...], jnp.concatenate(halves, axis=0))
    upper, lower = (banded[:, n * HD : (n + 1) * HD].reshape(BANDS, WIDE, 8, HD) for n in range(2))
    rows = jnp.concatenate([upper, lower], axis=2).astype(jnp.bfloat16)
    out_ref[...] = rows.reshape(BANDS, WIDE * 16, HD)


def combine(mine, other):
    choose = jnp.asarray(band_selection(), jnp.bfloat16)
    return pl.pallas_call(
        combine_kernel,
        grid=(2,),
        in_specs=[pl.BlockSpec(memory_space=pltpu.VMEM)] * 3,
        out_specs=pl.BlockSpec((BANDS, WIDE * 16, HD), lambda i: (i, 0, 0)),
        out_shape=jax.ShapeDtypeStruct((2 * BANDS, WIDE * 16, HD), jnp.bfloat16),
        compiler_params=pltpu.CompilerParams(vmem_limit_bytes=20 * MIB),
    )(mine, other, choose)


def window_selection():
    chosen = np.zeros((3, 4 * C_LAT, 2, 4, C_LAT), np.float32)
    for i in range(2):
        for col in range(4):
            side, j = divmod(col + 1, 2)
            for ch in range(C_LAT):
                chosen[side, 4 * ch + 2 * i + j, i, col, ch] = 1.0
    return chosen.reshape(3, 4 * C_LAT, 128)


def row_order():
    chosen = np.zeros((BAND, PH, BAND, PH), np.float32)
    for col in range(BAND):
        for row in range(PH):
            pair, core, low = (row // 4, row // 2 % 2, row % 2)
            chosen[col, row, col, core * 16 + pair * 2 + low] = 1.0
    return chosen.reshape(BAND * PH, BAND * PH)


TILE_N = 512
AHEAD = 4


def project_kernel(
    band_ref, x_ref, w_ref, shift_ref, scale_ref, final_ref, choose_ref, order_ref, out_ref, rows_ref, proj_ref, tiles_ref, sems
):
    tiles = D // TILE_N

    def fetch(n):
        return pltpu.make_async_copy(w_ref.at[:, pl.ds(n * TILE_N, TILE_N)], tiles_ref.at[n], sems.at[n])

    for n in range(AHEAD):
        fetch(n).start()
    for head in range(HEADS):
        for core in range(2):
            for col in range(WIDE):
                at = col * PH + core * 16
                rows_ref[at : at + 16, head * HD : (head + 1) * HD] = x_ref[head, core, col * 16 : (col + 1) * 16, :]
    total = 0.0
    square = 0.0
    for n in range(tiles):
        fetch(n).wait()
        if n + AHEAD < tiles:
            fetch(n + AHEAD).start()
        part = jnp.dot(rows_ref[...], tiles_ref[n], preferred_element_type=jnp.float32)
        proj_ref[n] = part
        part_sum = jnp.sum(part, axis=1, keepdims=True)
        if n == 0:
            near = part_sum / TILE_N
        total = total + part_sum
        square = square + jnp.sum((part - near) * (part - near), axis=1, keepdims=True)
    mean = total / D
    variance = square / D - (mean - near) * (mean - near)
    inverse = 1.0 / jnp.sqrt(variance + 1e-06)

    def reduce(n, patches):
        at = slice(n * TILE_N, (n + 1) * TILE_N)
        normed = (proj_ref[n] - mean) * inverse * (1.0 + scale_ref[:, at]) + shift_ref[:, at]
        return patches + jnp.dot(normed.astype(jnp.bfloat16), final_ref[at, :], preferred_element_type=jnp.float32)

    patches = jnp.zeros((PH * WIDE, 4 * C_LAT), jnp.float32)
    for n in range(tiles):
        patches = reduce(n, patches)
    place = lax.broadcasted_iota(jnp.int32, patches.shape, 0) // PH + (band_ref[0] * BAND - 1)
    patches = jnp.where((place >= 0) & (place < PW), patches, 0.0).astype(jnp.bfloat16)
    wide = 0.0
    for side in range(3):
        moved = patches[side * PH : (side + BAND) * PH]
        wide = wide + jnp.dot(moved, choose_ref[side], preferred_element_type=jnp.float32)
    wide = jnp.dot(order_ref[...], wide.astype(jnp.bfloat16), preferred_element_type=jnp.float32)
    out_ref[...] = wide.astype(jnp.bfloat16)


def project(band, gathered, w_out, shift_vec, scale_vec, w_final):
    choose = jnp.asarray(window_selection(), jnp.bfloat16)
    order = jnp.asarray(row_order(), jnp.bfloat16)
    vmem = pl.BlockSpec(memory_space=pltpu.VMEM)
    return pl.pallas_call(
        project_kernel,
        in_specs=[pl.BlockSpec(memory_space=pltpu.SMEM), vmem, pl.BlockSpec(memory_space=pl.ANY)] + [vmem] * 5,
        out_specs=vmem,
        out_shape=jax.ShapeDtypeStruct((BAND * PH, 128), jnp.bfloat16),
        scratch_shapes=[
            pltpu.VMEM((PH * WIDE, HEADS * HD), jnp.bfloat16),
            pltpu.VMEM((D // TILE_N, PH * WIDE, TILE_N), jnp.float32),
            pltpu.VMEM((D // TILE_N, HEADS * HD, TILE_N), jnp.bfloat16),
            pltpu.SemaphoreType.DMA((D // TILE_N,)),
        ],
        compiler_params=pltpu.CompilerParams(vmem_limit_bytes=52 * MIB),
    )(band, gathered, w_out, shift_vec.reshape(1, D), scale_vec.reshape(1, D), w_final, choose, order)


def windows_of(grid, odd):
    rows = BAND * PH
    row = lax.rem(lax.broadcasted_iota(jnp.int32, (rows, 128), 0), PH)
    if odd == 0:
        beside = jnp.where(row == 0, 0.0, pltpu.roll(grid, 1, 0))
    else:
        beside = jnp.where(row == PH - 1, 0.0, pltpu.roll(grid, rows - 1, 0))
    return jnp.concatenate([grid, beside], axis=1).astype(jnp.bfloat16)


def conv_now_kernel(now_ref, w_ref, part_ref, taps_ref, last_ref):
    for taps, frames in ((taps_ref, (0, 1)), (last_ref, (2,))):
        taps[...] = jnp.zeros_like(taps)
        for odd in range(2):
            for n, a in enumerate(frames):
                for b in range(3):
                    y = odd + b - 1
                    offset = {-1: 192, 0: 0, 1: 64, 2: 128}[y]
                    for j in range(2):
                        for e in range(3):
                            at = offset + (j + e) * C_LAT
                            tap = ((a * 3 + b) * 3 + e) * C_LAT
                            taps[odd, n, at : at + C_LAT, j * C_VAE : (j + 1) * C_VAE] = w_ref[tap : tap + C_LAT, :]
    now = now_ref[...].astype(jnp.float32)
    for odd in range(2):
        part_ref[odd] = jnp.dot(windows_of(now, odd), last_ref[odd, 0], preferred_element_type=jnp.float32)


def conv_kernel(frame_ref, now_ref, one_ref, two_ref, part_ref, taps_ref, out_ref, spread_ref):
    width = out_ref.shape[2]
    start = pl.program_id(0) * width
    frame = frame_ref[0]
    now = now_ref[...].astype(jnp.float32)
    one = jnp.where(frame >= 1, one_ref[...].astype(jnp.float32), now)
    two = jnp.where(frame >= 2, two_ref[...].astype(jnp.float32), one)
    for odd in range(2):
        windows = [windows_of(grid, odd) for grid in (two, one)]
        for j in range(2):
            lanes = pl.ds(pl.multiple_of(j * C_VAE + start, width), width)
            result = part_ref[odd, :, lanes]
            for a in range(2):
                result = result + jnp.dot(windows[a], taps_ref[odd, a, :, lanes], preferred_element_type=jnp.float32)
            for col in range(BAND):
                for part in range(width // 128):
                    spread_ref[part, pl.ds((2 * col + j) * 2 * PH + odd, PH, stride=2), :] = result[
                        col * PH : (col + 1) * PH, part * 128 : (part + 1) * 128
                    ]
    for part in range(width // 128):
        final = spread_ref[part].reshape(2 * BAND, 2 * PH, 128)
        out_ref[:, :, part * 128 : (part + 1) * 128] = final.astype(jnp.bfloat16)


def convolve(frame, now, one, two, w_conv):
    rows = BAND * PH
    vmem = pl.BlockSpec(memory_space=pltpu.VMEM)
    taps = w_conv.reshape(27 * C_LAT, C_VAE)
    part, taps = pl.pallas_call(
        conv_now_kernel,
        in_specs=[vmem] * 2,
        out_specs=[vmem] * 2,
        out_shape=[
            jax.ShapeDtypeStruct((2, rows, 2 * C_VAE), jnp.float32),
            jax.ShapeDtypeStruct((2, 2, 256, 2 * C_VAE), jnp.bfloat16),
        ],
        scratch_shapes=[pltpu.VMEM((2, 1, 256, 2 * C_VAE), jnp.bfloat16)],
        compiler_params=pltpu.CompilerParams(vmem_limit_bytes=24 * MIB),
        cost_estimate=pl.CostEstimate(flops=rows * 2 ** 20, bytes_accessed=2 ** 22, transcendentals=0),
    )(now, taps)
    return pl.pallas_call(
        conv_kernel,
        grid=(2,),
        in_specs=[pl.BlockSpec(memory_space=pltpu.SMEM)] + [vmem] * 5,
        out_specs=pl.BlockSpec((2 * BAND, 2 * PH, C_VAE // 2), lambda i: (0, 0, i)),
        out_shape=jax.ShapeDtypeStruct((2 * BAND, 2 * PH, C_VAE), jnp.bfloat16),
        scratch_shapes=[pltpu.VMEM((C_VAE // 256, 4 * BAND * PH, 128), jnp.float32)],
        compiler_params=pltpu.CompilerParams(vmem_limit_bytes=24 * MIB),
    )(frame, now, one, two, part, taps)


def ring(x, axis, by):
    count = lax.axis_size(axis)
    return lax.ppermute(x, axis, [(i, (i + by) % count) for i in range(count)])


def later(x, by):
    count = lax.axis_size(("y", "zl"))
    return lax.ppermute(x, ("y", "zl"), [(i, i + by) for i in range(count - by)])


def per_device(queries, key_rows, value_rows, w_out, shift_vec, scale_vec, w_final, w_conv):
    tokens = queries.shape[0]

    def by_head(x):
        return x.reshape(tokens, HEADS, HD).transpose(1, 0, 2)

    outgoing = jnp.concatenate([by_head(key_rows), by_head(value_rows), by_head(queries)], axis=2)
    incoming = lax.all_to_all(outgoing, PLANE, 0, 0, tiled=True).reshape(HEADS * tokens, 3 * HD)
    half = HEADS * tokens // 2
    kv = incoming[:, : 2 * HD]
    kv_a, kv_b = (kv[:half], kv[half:])
    q_mine = incoming[:, 2 * HD :]
    below_a, above_b = (ring(kv_a, "y", 1), ring(kv_b, "y", -1))
    q_theirs = ring(q_mine, "c", 1)
    columns = 4 * half
    state = attend(q_mine, [kv_a, kv_b], columns=columns)
    kv_a, kv_b, q_theirs, state = lax.optimization_barrier((kv_a, kv_b, q_theirs, state))
    below_b, above_a = (ring(kv_b, "y", 1), ring(kv_a, "y", -1))
    state = attend(q_theirs, [kv_a, kv_b], columns=columns, offset=2 * half, fill=state)
    q_all = jnp.concatenate([q_mine, q_theirs], axis=0)
    below_a, above_b, state = lax.optimization_barrier((below_a, above_b, state))
    far_a, far_b = (ring(below_a, "y", 1), ring(above_b, "y", -1))
    state = attend(q_all, [below_a, above_b], state)
    below_b, above_a, state = lax.optimization_barrier((below_b, above_a, state))
    state = attend(q_all, [below_b, above_a], state)
    far_a, far_b, state = lax.optimization_barrier((far_a, far_b, state))
    theirs = attend(q_theirs, [far_a, far_b], state, offset=2 * half)
    theirs = ring(theirs, "c", 1)
    mine = attend(q_mine, [far_a, far_b], state)
    banded = combine(mine, theirs)
    gathered = lax.all_to_all(banded, ("zl", "x", "zh", "c"), 0, 0, tiled=True)
    gathered = gathered.reshape(HEADS, 2, WIDE * 16, HD)
    band = lax.axis_index(("x", "zh", "c")).astype(jnp.int32).reshape(1)
    frame = lax.axis_index(("y", "zl")).astype(jnp.int32).reshape(1)
    now = project(band, gathered, w_out, shift_vec, scale_vec, w_final)
    decoded = convolve(frame, now, later(now, 1), later(now, 2), w_conv)
    return decoded.transpose(1, 0, 2)[None]


def solution(mesh):
    fine = Mesh(mesh.devices.reshape(SIZES), AXES)
    rows = P(AXES, None)
    return jax.shard_map(
        per_device,
        mesh=fine,
        in_specs=(rows, rows, rows, P(), P(), P(), P(), P()),
        out_specs=P(("y", "zl"), None, ("x", "zh", "c"), None),
        check_vma=False,
    )
```
